32 devices in a mesh: seq: 4 (over z), dp: 2 (over core), head: 4 (over y, x).
Axes of the slice: x: 2, y: 2, z: 4, core: 2. Of those that a mesh axis runs over, the one named last changes fastest.
Arguments:
- inputs: bfloat16 [2, 1536, 3072], P('dp', 'seq'), may hold values from -40 to 40
- w_query: bfloat16 [3072, 2048], P(None, 'head'), may hold values from -0.21650635 to 0.21650635
- w_key: bfloat16 [3072, 2048], P(None, 'head'), may hold values from -0.07216878 to 0.07216878
- w_value: bfloat16 [3072, 2048], P(None, 'head'), may hold values from -0.108253175 to 0.108253175
- gate_bias: float32 [8], P('head'), may hold values from 0 to 2.5
- cotangent: bfloat16 [2, 1536, 2048], P('dp', 'seq', 'head'), may hold values from -8 to 8
Outputs:
- blended: bfloat16 [2, 1536, 2048], P('dp', 'seq', 'head')
- grad_weights: float32 [3072, 3, 2048], P(('seq', 'dp'), None, 'head')
The draws below stay inside these ranges and needn't reach their ends.
All inputs are finite; a program needn't handle non-finite values.
Results may differ from the reference program's by a relative error of at most 0.012.
Values may be sent and summed in bfloat16 or wider, within the bound.
No kernel may reach another device: no remote copies, remote signals or barrier semaphores. Data moves between devices by JAX's collectives and lax.ppermute only.
A program may use at most 128 MiB of HBM per device.

```python
import math
import jax
import jax.numpy as jnp
from jax import lax

D = 3072
HEADS = 8
HDIM = 256
SEG = 384
BATCH = 2
LENGTH = 1536


def shared_mean(key):
    raw = jax.random.normal(jax.random.fold_in(key, 101), (D,), jnp.float32)
    return jnp.clip(raw, -4.0, 4.0)


def remove_mean(matrix, mean_row):
    along = jnp.dot(mean_row, matrix, precision=lax.Precision.HIGHEST) / jnp.sum(mean_row * mean_row)
    return matrix - mean_row[:, None] * along[None, :]


def key_basis(key):
    mean_row = shared_mean(key)
    raw = jnp.clip(jax.random.normal(jax.random.fold_in(key, 202), (D, HEADS * HDIM), jnp.float32), -6.0, 6.0)
    return remove_mean(raw, mean_row) / math.sqrt(D)


def draw_inputs(key, part):
    subkeys = jax.random.split(jax.random.fold_in(key, 11), 2)
    segments = LENGTH // SEG
    mean_row = shared_mean(key)
    common = jax.random.normal(subkeys[1], (BATCH, segments, 1, D), jnp.float32)
    noise_part = jax.random.normal(subkeys[0], (BATCH, segments, SEG, D), jnp.float32)
    mixed_rows = mean_row + 0.5 * common + noise_part
    return jnp.clip(mixed_rows.reshape(BATCH, LENGTH, D), -40.0, 40.0).astype(jnp.bfloat16)


def draw_w_query(key, part):
    mean_row = shared_mean(key)
    raw = jnp.clip(jax.random.normal(jax.random.fold_in(key, 303), (D, HEADS * HDIM), jnp.float32), -6.0, 6.0)
    offsets = jax.random.uniform(jax.random.fold_in(key, 404), (HEADS * HDIM,), jnp.float32, -5.0, -3.0)
    weight = 1.8 * remove_mean(raw, mean_row) / math.sqrt(D)
    weight = weight + mean_row[:, None] * offsets[None, :] / jnp.sum(mean_row * mean_row)
    limit = 12.0 / math.sqrt(D)
    return jnp.clip(weight, -limit, limit).astype(jnp.bfloat16)


def draw_w_key(key, part):
    weight = 0.58 * key_basis(key)
    limit = 4.0 / math.sqrt(D)
    return jnp.clip(weight, -limit, limit).astype(jnp.bfloat16)


def draw_w_value(key, part):
    basis = key_basis(key).reshape(D, HEADS, HDIM)
    mixer = jax.random.normal(jax.random.fold_in(key, 505), (HEADS, HDIM, HDIM), jnp.float32) / math.sqrt(HDIM)
    linked = jnp.einsum('chd,hde->che', basis, mixer, precision=lax.Precision.HIGHEST).reshape(D, HEADS * HDIM)
    mean_row = shared_mean(key)
    raw = jnp.clip(jax.random.normal(jax.random.fold_in(key, 606), (D, HEADS * HDIM), jnp.float32), -6.0, 6.0)
    weight = 0.9 * linked + 0.436 * remove_mean(raw, mean_row) / math.sqrt(D)
    limit = 6.0 / math.sqrt(D)
    return jnp.clip(weight, -limit, limit).astype(jnp.bfloat16)


def steps_of(stream_key, shape, cuts, low, largest):
    level = 1.0
    for axis_at, blocks in cuts:
        steps = jax.random.uniform(jax.random.fold_in(jax.random.fold_in(stream_key, 6), axis_at), (blocks,), jnp.float32, low / len(cuts), largest / len(cuts))
        level = level * jnp.repeat(jnp.exp(steps), shape[axis_at] // blocks).reshape((-1,) + (1,) * (len(shape) - 1 - axis_at))
    return level


def normal_values(rng, extent, width, reach, cuts=(), held_as=jnp.bfloat16):
    values = width * jax.random.normal(rng, extent, jnp.float32)
    if cuts:
        values = values * steps_of(rng, extent, cuts, -0.22, 0.18)
    return jnp.clip(values, -reach, reach).astype(held_as)


def setup_inputs(seed: int = 0) -> dict:
    key_of = jax.random.split(jax.random.key(seed), 7)
    return {
        "inputs": draw_inputs(jax.random.fold_in(key_of[6], 71), 0),
        "w_query": draw_w_query(jax.random.fold_in(key_of[6], 71), 0),
        "w_key": draw_w_key(jax.random.fold_in(key_of[6], 71), 0),
        "w_value": draw_w_value(jax.random.fold_in(key_of[6], 71), 0),
        "gate_bias": jnp.clip(2.5 * jax.random.uniform(key_of[4], (HEADS,), jnp.float32) ** steps_of(key_of[4], (HEADS,), ((0, 4),), -0.2, 0.2), 0.0, 2.5),
        "cotangent": normal_values(key_of[5], (BATCH, LENGTH, HEADS * HDIM), 1.0, 8.0, ((0, 2), (1, 4), (2, 4))),
    }


exact_mode = lax.Precision.HIGHEST

def product(form, left, right):
    return jnp.einsum(form, left.astype(jnp.float32), right.astype(jnp.float32))

def feature(values_in):
    return jnp.where(values_in > 0, values_in + 1.0, jnp.exp(jnp.minimum(values_in, 0.0)))

def feature_slope(values_in):
    return jnp.where(values_in > 0, 1.0, jnp.exp(jnp.minimum(values_in, 0.0)))

def write_memory(keys_own, values_own):
    phi_key = feature(keys_own.astype(jnp.float32))
    memory = jnp.einsum('shd,she->hde', phi_key, values_own.astype(jnp.float32), precision=exact_mode)
    return (memory, lax.optimization_barrier(jnp.sum(phi_key, axis=0)))

def write_grads(keys_own, values_own, grad_memory, grad_norm):
    key_float = keys_own.astype(jnp.float32)
    phi_key = feature(key_float)
    grad_phi = jnp.einsum('hde,she->shd', grad_memory, values_own.astype(jnp.float32), precision=exact_mode) + grad_norm[None]
    grad_value = jnp.einsum('shd,hde->she', phi_key, grad_memory, precision=exact_mode)
    return (grad_phi * feature_slope(key_float), grad_value)

def attend(queries, keys_own, values_own, keys_prev, values_prev, has_prev, memory, normaliser, gate_bias):
    seg_len, head_count, head_dim = queries.shape
    all_keys = jnp.concatenate([keys_prev, keys_own], 0)
    all_values = jnp.concatenate([values_prev, values_own], 0)
    score_scale = head_dim ** (-0.5)
    scores = product('shd,thd->hst', queries, all_keys) * score_scale
    row_ids = lax.broadcasted_iota(jnp.int32, (seg_len, 2 * seg_len), 0)
    col_ids = lax.broadcasted_iota(jnp.int32, (seg_len, 2 * seg_len), 1)
    allowed = (col_ids <= row_ids + seg_len) & ((col_ids >= seg_len) | has_prev)
    scores = jnp.where(allowed[None], scores, -1e+30)
    row_max = lax.optimization_barrier(jnp.max(scores, axis=2, keepdims=True))
    weights = jnp.exp(scores - row_max)
    softmax = weights / lax.optimization_barrier(jnp.sum(weights, axis=2, keepdims=True))
    soft_bf = softmax.astype(jnp.bfloat16)
    local_out = product('hst,thd->shd', soft_bf, all_values)
    phi_query = feature(queries.astype(jnp.float32))
    numerator = jnp.einsum('shd,hde->she', phi_query, memory, precision=exact_mode)
    denominator = jnp.einsum('shd,hd->sh', phi_query, normaliser, precision=exact_mode) + 1.0
    retrieved = numerator / denominator[:, :, None]
    mixing = jax.nn.sigmoid(gate_bias)[None, :, None]
    blended = mixing * retrieved + (1.0 - mixing) * local_out
    stored = (all_keys, all_values, softmax, soft_bf, phi_query, retrieved, denominator)
    return (blended.astype(jnp.bfloat16), stored)

def backprop(cotangent, queries, memory, normaliser, gate_bias, stored):
    all_keys, all_values, softmax, soft_bf, phi_query, retrieved, denominator = stored
    head_dim = queries.shape[2]
    mixing = jax.nn.sigmoid(gate_bias)[None, :, None]
    upstream = cotangent.astype(jnp.float32)
    grad_ret = mixing * upstream
    grad_local = ((1.0 - mixing) * upstream).astype(jnp.bfloat16)
    grad_soft = product('shd,thd->hst', grad_local, all_values)
    grad_values = product('hst,shd->thd', soft_bf, grad_local)
    row_dot = lax.optimization_barrier(jnp.sum(softmax * grad_soft, axis=2, keepdims=True))
    grad_scores = (softmax * (grad_soft - row_dot) * head_dim ** (-0.5)).astype(jnp.bfloat16)
    grad_query = product('hst,thd->shd', grad_scores, all_keys)
    grad_keys = product('hst,shd->thd', grad_scores, queries)
    grad_num = grad_ret / denominator[:, :, None]
    grad_den = -lax.optimization_barrier(jnp.sum(grad_ret * retrieved, axis=2)) / denominator
    grad_phi = jnp.einsum('she,hde->shd', grad_num, memory, precision=exact_mode) + grad_den[:, :, None] * normaliser[None]
    grad_memory = jnp.einsum('shd,she->hde', phi_query, grad_num, precision=exact_mode)
    grad_norm = jnp.einsum('shd,sh->hd', phi_query, grad_den, precision=exact_mode)
    grad_query = grad_query + grad_phi * feature_slope(queries.astype(jnp.float32))
    return (grad_query, grad_keys, grad_values, grad_memory, grad_norm)

def prefix_before(stacked):
    running = jnp.cumsum(stacked, axis=0)
    return jnp.concatenate([jnp.zeros_like(running[:1]), running[:-1]], 0)

def suffix_after(stacked):
    running = jnp.cumsum(stacked[::-1], axis=0)[::-1]
    return jnp.concatenate([running[1:], jnp.zeros_like(running[:1])], 0)

def one_sequence(tokens, w_query, w_key, w_value, gate_bias, cotangent):
    length = tokens.shape[0]
    head_count = gate_bias.shape[0]
    columns = w_query.shape[1]
    head_dim = columns // head_count
    blocks = length // SEG

    def project(weight):
        flat = jnp.dot(tokens, weight, preferred_element_type=jnp.float32).astype(jnp.bfloat16)
        return flat.reshape(blocks, SEG, head_count, head_dim)
    queries = project(w_query)
    keys_all = project(w_key)
    values_all = project(w_value)
    memories, norms_all = jax.vmap(write_memory)(keys_all, values_all)
    memory_prev = prefix_before(memories)
    norm_prev = prefix_before(norms_all)
    keys_prev = jnp.concatenate([jnp.zeros_like(keys_all[:1]), keys_all[:-1]], 0)
    values_prev = jnp.concatenate([jnp.zeros_like(values_all[:1]), values_all[:-1]], 0)
    has_prev = jnp.arange(blocks) > 0
    cot_blocks = cotangent.reshape(blocks, SEG, head_count, head_dim)

    def segment(pieces):
        query_block, key_block, value_block, key_before, value_before, flag_prev, memory_in, normaliser_in, cot_block = pieces
        out_block, stored = attend(query_block, key_block, value_block, key_before, value_before, flag_prev, memory_in, normaliser_in, gate_bias)
        grads = backprop(cot_block, query_block, memory_in, normaliser_in, gate_bias, stored)
        return (out_block,) + grads
    outputs, grad_query, grad_keys, grad_values, grad_memory, grad_norm = lax.map(segment, (queries, keys_all, values_all, keys_prev, values_prev, has_prev, memory_prev, norm_prev, cot_blocks))
    grad_mem_seg = suffix_after(grad_memory)
    grad_norm_seg = suffix_after(grad_norm)
    write_key, write_value = jax.vmap(write_grads)(keys_all, values_all, grad_mem_seg, grad_norm_seg)
    halo_keys = grad_keys[:, :SEG].astype(jnp.bfloat16)
    halo_values = grad_values[:, :SEG].astype(jnp.bfloat16)
    next_keys = jnp.concatenate([halo_keys[1:], jnp.zeros_like(halo_keys[:1])], 0)
    next_values = jnp.concatenate([halo_values[1:], jnp.zeros_like(halo_values[:1])], 0)
    grad_key = (grad_keys[:, SEG:] + next_keys.astype(jnp.float32) + write_key).astype(jnp.bfloat16)
    grad_value = (grad_values[:, SEG:] + next_values.astype(jnp.float32) + write_value).astype(jnp.bfloat16)
    grad_all = jnp.concatenate([grad_query.astype(jnp.bfloat16).reshape(length, columns), grad_key.reshape(length, columns), grad_value.reshape(length, columns)], 1)
    weight_term = jnp.dot(tokens.T, grad_all, preferred_element_type=jnp.float32)
    return (outputs.reshape(length, columns), weight_term)

def reference(inputs, w_query, w_key, w_value, gate_bias, cotangent):
    results = []
    grad_total = None
    for batch_index in range(BATCH):
        output_one, weight_term = one_sequence(inputs[batch_index], w_query, w_key, w_value, gate_bias, cotangent[batch_index])
        results.append(output_one)
        grad_total = weight_term if grad_total is None else grad_total + weight_term
    grad_scale = 1.0 / math.sqrt(BATCH * LENGTH)
    grad_weights = (grad_total * grad_scale).reshape(D, 3, HEADS * HDIM)
    return (jnp.stack(results, 0), grad_weights)
```

```python
import functools
import math

import jax
import jax.numpy as jnp
from jax import lax
from jax.experimental import pallas as pl
from jax.experimental.pallas import tpu as pltpu
from jax.sharding import PartitionSpec as P

VMEM_LIMIT = 48 * 1024 * 1024


def dot_nn(left, right):
    return lax.dot_general(
        left, right, (((1,), (0,)), ((), ())), preferred_element_type=jnp.float32
    )


def dot_nt(left, right):
    return lax.dot_general(
        left, right, (((1,), (1,)), ((), ())), preferred_element_type=jnp.float32
    )


def dot_tn(left, right):
    return lax.dot_general(
        left, right, (((0,), (0,)), ((), ())), preferred_element_type=jnp.float32
    )


def halves(value):
    high = value.astype(jnp.bfloat16)
    low = (value - high.astype(jnp.float32)).astype(jnp.bfloat16)
    return high, low


def wide(dot, left, right):
    left_high, left_low = halves(left)
    right_high, right_low = halves(right)
    return dot(left_high, right_high) + (dot(left_high, right_low) + dot(left_low, right_high))


def feature(value):
    return jnp.where(value > 0, value + 1.0, jnp.exp(jnp.minimum(value, 0.0)))


def feature_slope(value):
    return jnp.where(value > 0, 1.0, jnp.exp(jnp.minimum(value, 0.0)))


def write_kernel(key_ref, value_ref, memory_ref, norm_ref):
    phi_key = feature(key_ref[...].astype(jnp.float32))
    high, low = halves(phi_key)
    value = value_ref[...]
    memory_ref[0] = dot_tn(high, value) + dot_tn(low, value)
    norm_ref[...] = jnp.sum(phi_key, axis=0, keepdims=True)


def grad_memory_kernel(query_ref, cot_ref, norm_ref, mix_ref, out_ref):
    phi_query = feature(query_ref[...].astype(jnp.float32))
    denominator = jnp.sum(phi_query * norm_ref[...], axis=1, keepdims=True) + 1.0
    grad_num = mix_ref[...] * cot_ref[...].astype(jnp.float32) / denominator
    out_ref[0] = wide(dot_tn, phi_query, grad_num)


def attend_kernel(
    has_prev_ref,
    query_ref,
    key_ref,
    value_ref,
    key_prev_ref,
    value_prev_ref,
    cot_ref,
    mix_ref,
    out_ref,
    grad_query_ref,
    stats_ref,
):
    query = query_ref[...]
    seg_len, head_dim = query.shape
    scale = head_dim ** (-0.5)
    key, key_prev = key_ref[...], key_prev_ref[...]
    value, value_prev = value_ref[...], value_prev_ref[...]
    rows = lax.broadcasted_iota(jnp.int32, (seg_len, seg_len), 0)
    cols = lax.broadcasted_iota(jnp.int32, (seg_len, seg_len), 1)
    score_own = jnp.where(cols <= rows, dot_nt(query, key) * scale, -1e30)
    score_prev = jnp.where(has_prev_ref[0] > 0, dot_nt(query, key_prev) * scale, -1e30)
    row_max = jnp.maximum(
        jnp.max(score_own, axis=1, keepdims=True), jnp.max(score_prev, axis=1, keepdims=True)
    )
    weight_own = jnp.exp(score_own - row_max)
    weight_prev = jnp.exp(score_prev - row_max)
    inverse = 1.0 / (
        jnp.sum(weight_own, axis=1, keepdims=True) + jnp.sum(weight_prev, axis=1, keepdims=True)
    )
    soft_own = weight_own * inverse
    soft_prev = weight_prev * inverse
    out_ref[...] = dot_nn(soft_own.astype(jnp.bfloat16), value) + dot_nn(
        soft_prev.astype(jnp.bfloat16), value_prev
    )
    grad_local = ((1.0 - mix_ref[...]) * cot_ref[...].astype(jnp.float32)).astype(jnp.bfloat16)
    grad_own = dot_nt(grad_local, value)
    grad_prev = dot_nt(grad_local, value_prev)
    row_dot = jnp.sum(soft_own * grad_own, axis=1, keepdims=True) + jnp.sum(
        soft_prev * grad_prev, axis=1, keepdims=True
    )
    score_grad_own = (soft_own * (grad_own - row_dot) * scale).astype(jnp.bfloat16)
    score_grad_prev = (soft_prev * (grad_prev - row_dot) * scale).astype(jnp.bfloat16)
    grad_query_ref[...] = dot_nn(score_grad_own, key) + dot_nn(score_grad_prev, key_prev)
    lane = lax.broadcasted_iota(jnp.int32, (seg_len, 128), 1)
    stats = jnp.where(
        lane == 0, row_max, jnp.where(lane == 1, inverse, jnp.where(lane == 2, row_dot, 0.0))
    )
    stats_ref[...] = jnp.transpose(stats)[:8]


def retrieve_kernel(
    query_ref,
    cot_ref,
    memory_ref,
    norm_ref,
    mix_ref,
    local_ref,
    grad_att_ref,
    blended_ref,
    grad_query_ref,
    grad_norm_ref,
):
    query = query_ref[...].astype(jnp.float32)
    phi_query = feature(query)
    norm = norm_ref[...]
    memory = memory_ref[0]
    mix = mix_ref[...]
    denominator = jnp.sum(phi_query * norm, axis=1, keepdims=True) + 1.0
    retrieved = wide(dot_nn, phi_query, memory) / denominator
    blended = mix * retrieved + (1.0 - mix) * local_ref[...]
    blended_ref[...] = blended.astype(jnp.bfloat16)
    grad_ret = mix * cot_ref[...].astype(jnp.float32)
    grad_num = grad_ret / denominator
    grad_den = -jnp.sum(grad_ret * retrieved, axis=1, keepdims=True) / denominator
    grad_phi = wide(dot_nt, grad_num, memory) + grad_den * norm
    grad_norm_ref[...] = jnp.sum(grad_den * phi_query, axis=0, keepdims=True)
    grad_query = grad_att_ref[...] + grad_phi * feature_slope(query)
    grad_query_ref[...] = grad_query.astype(jnp.bfloat16)


def key_value_kernel(
    key_ref,
    value_ref,
    query_ref,
    cot_ref,
    stats_ref,
    query_next_ref,
    cot_next_ref,
    stats_next_ref,
    grad_memory_ref,
    mix_ref,
    grad_key_ref,
    grad_value_ref,
):
    key, value = key_ref[...], value_ref[...]
    seg_len, head_dim = key.shape
    scale = head_dim ** (-0.5)
    keep = 1.0 - mix_ref[...]

    def part(query, cot, stats, causal):
        grad_local = (keep * cot.astype(jnp.float32)).astype(jnp.bfloat16)
        score = dot_nt(key, query) * scale
        if causal:
            rows = lax.broadcasted_iota(jnp.int32, score.shape, 0)
            cols = lax.broadcasted_iota(jnp.int32, score.shape, 1)
            score = jnp.where(rows <= cols, score, -1e30)
        soft = jnp.exp(score - stats[0:1]) * stats[1:2]
        grad_value = dot_nn(soft.astype(jnp.bfloat16), grad_local)
        grad_soft = dot_nt(value, grad_local)
        score_grad = (soft * (grad_soft - stats[2:3]) * scale).astype(jnp.bfloat16)
        return dot_nn(score_grad, query), grad_value

    own_key, own_value = part(query_ref[...], cot_ref[...], stats_ref[...], True)
    next_key, next_value = part(query_next_ref[...], cot_next_ref[...], stats_next_ref[...], False)
    key_float = key.astype(jnp.float32)
    high, low = halves(grad_memory_ref[0])
    phi_high, phi_low = halves(feature(key_float))
    from_memory = dot_nt(value, high) + dot_nt(value, low)
    grad_key_ref[...] = own_key + next_key + from_memory * feature_slope(key_float)
    to_value = dot_nn(phi_high, high) + (dot_nn(phi_high, low) + dot_nn(phi_low, high))
    grad_value_ref[...] = (own_value + next_value + to_value).astype(jnp.bfloat16)


def call(kernel, heads, seg_len, head_dim, ins, outs, flops):
    specs = {
        "f": pl.BlockSpec(memory_space=pltpu.SMEM),
        "c": pl.BlockSpec((seg_len, head_dim), lambda h: (0, h)),
        "r": pl.BlockSpec((1, head_dim), lambda h: (0, h)),
        "m": pl.BlockSpec((1, head_dim, head_dim), lambda h: (h, 0, 0)),
        "s": pl.BlockSpec((8, seg_len), lambda h: (h, 0)),
    }
    shapes = {
        "c": (seg_len, heads * head_dim),
        "r": (1, heads * head_dim),
        "m": (heads, head_dim, head_dim),
        "s": (8 * heads, seg_len),
    }
    return pl.pallas_call(
        kernel,
        grid=(heads,),
        in_specs=[specs[kind] for kind in ins],
        out_specs=[specs[kind] for kind, _ in outs],
        out_shape=[jax.ShapeDtypeStruct(shapes[kind], dtype) for kind, dtype in outs],
        compiler_params=pltpu.CompilerParams(vmem_limit_bytes=VMEM_LIMIT),
        cost_estimate=pl.CostEstimate(
            flops=flops, bytes_accessed=4 * 1024 * 1024, transcendentals=0
        ),
    )


def local(inputs, w_query, w_key, w_value, gate_bias, cotangent):
    tokens = inputs[0]
    cot = cotangent[0]
    seg_len, model_dim = tokens.shape
    heads = gate_bias.shape[0]
    columns = w_query.shape[1]
    head_dim = columns // heads
    seq_count, seq_at = lax.axis_size("seq"), lax.axis_index("seq")
    dp_count, dp_at = lax.axis_size("dp"), lax.axis_index("dp")
    part_rows = model_dim // (seq_count * dp_count)
    f32, bf16 = jnp.float32, jnp.bfloat16

    def shifted(x, by, first=0, last=None):
        last = seq_count - 1 if last is None else last
        pairs = [
            (i, i + by) for i in range(first, last + 1) if 0 <= i + by < seq_count
        ]
        return lax.ppermute(x, "seq", pairs)

    def chain(own, by):
        total = jnp.zeros_like(own)
        for hop in range(seq_count - 1):
            at = hop if by > 0 else seq_count - 1 - hop
            total = total + shifted(total + own, by, at, at)
        return total

    def small_sums(own, by):
        total = jnp.zeros_like(own)
        for distance in range(1, seq_count):
            total = total + shifted(own, by * distance)
        return total

    def project(weight):
        return jnp.dot(tokens, weight, preferred_element_type=f32).astype(bf16)

    work = functools.partial(call, heads=heads, seg_len=seg_len, head_dim=head_dim)
    mix = jnp.repeat(jax.nn.sigmoid(gate_bias), head_dim)[None]
    has_prev = jnp.reshape((seq_at > 0).astype(jnp.int32), (1,))

    token_blocks = tokens.reshape(seg_len, seq_count, dp_count, part_rows)

    def rows_for(core):
        return lax.dynamic_index_in_dim(token_blocks, core, 2, False).reshape(
            seg_len, seq_count * part_rows
        )

    def from_core(x, step):
        return lax.ppermute(x, "dp", [(i, (i + step) % dp_count) for i in range(dp_count)])

    key = project(w_key)
    key_prev = shifted(key, 1)
    value = project(w_value)
    value_prev = shifted(value, 1)
    memory_own, norm_own = work(
        write_kernel, ins="cc", outs=(("m", f32), ("r", f32)), flops=3 * 10**8
    )(key, value)
    norm = small_sums(norm_own, 1)
    memory = chain(memory_own, 1)
    cot_next = shifted(cot, -1)
    query = project(w_query)
    query_next = shifted(query, -1)
    (grad_memory_own,) = work(
        grad_memory_kernel, ins="ccrr", outs=(("m", f32),), flops=3 * 10**8
    )(query, cot, norm, mix)
    grad_memory = chain(grad_memory_own, -1)

    token_parts = [rows_for(dp_at)] + [
        from_core(rows_for((dp_at + step) % dp_count), step) for step in range(1, dp_count)
    ]

    local_out, grad_att, stats = work(
        attend_kernel,
        ins="fccccccr",
        outs=(("c", f32), ("c", f32), ("s", f32)),
        flops=2 * 10**9,
    )(has_prev, query, key, value, key_prev, value_prev, cot, mix)
    stats_next = shifted(stats, -1)
    blended, grad_query, grad_norm_own = work(
        retrieve_kernel,
        ins="ccmrrcc",
        outs=(("c", bf16), ("c", bf16), ("r", f32)),
        flops=6 * 10**8,
    )(query, cot, memory, norm, mix, local_out, grad_att)
    grad_norm = small_sums(grad_norm_own, -1)
    grad_key_rest, grad_value = work(
        key_value_kernel, ins="ccccsccsmr", outs=(("c", f32), ("c", bf16)), flops=2 * 10**9
    )(key, value, query, cot, stats, query_next, cot_next, stats_next, grad_memory, mix)
    grad_key = (grad_key_rest + grad_norm * feature_slope(key.astype(f32))).astype(bf16)

    contract = (((0,), (0,)), ((), ()))
    grad_scale = 1.0 / math.sqrt(seq_count * dp_count * seg_len)

    def weight_term(grad):
        grads = [grad] + [from_core(grad, step) for step in range(1, dp_count)]
        total = None
        for rows, term in zip(token_parts, grads):
            product = lax.dot_general(rows, term, contract, preferred_element_type=f32)
            total = product if total is None else total + product
        terms = total.reshape(seq_count, part_rows, columns)

        def block(index):
            return lax.dynamic_index_in_dim(terms, jnp.clip(index, 0, seq_count - 1), 0, False)

        ups = jnp.zeros((part_rows, columns), bf16)
        downs = ups
        for turn in range(1, seq_count):
            ahead = seq_count - turn
            ups = shifted(
                (ups.astype(f32) + block(seq_at + ahead)).astype(bf16), 1, 0, turn - 1
            )
            downs = shifted(
                (downs.astype(f32) + block(seq_at - ahead)).astype(bf16), -1, ahead
            )
        return (ups.astype(f32) + downs.astype(f32) + block(seq_at)) * grad_scale

    pieces = [weight_term(grad) for grad in (grad_query, grad_key, grad_value)]
    return (blended[None], jnp.stack(pieces, 1))


def solution(mesh):
    return jax.shard_map(
        local,
        mesh=mesh,
        in_specs=(
            P("dp", "seq", None),
            P(None, "head"),
            P(None, "head"),
            P(None, "head"),
            P("head"),
            P("dp", "seq", "head"),
        ),
        out_specs=(P("dp", "seq", "head"), P(("seq", "dp"), None, "head")),
        check_vma=False,
    )
```

```python
import math

import jax
import jax.numpy as jnp
from jax import lax
from jax.experimental import pallas as pl
from jax.experimental.pallas import tpu as pltpu
from jax.sharding import PartitionSpec as P

VMEM_LIMIT = 48 * 1024 * 1024


def dot_nn(left, right):
    return lax.dot_general(
        left, right, (((1,), (0,)), ((), ())), preferred_element_type=jnp.float32
    )


def dot_nt(left, right):
    return lax.dot_general(
        left, right, (((1,), (1,)), ((), ())), preferred_element_type=jnp.float32
    )


def dot_tn(left, right):
    return lax.dot_general(
        left, right, (((0,), (0,)), ((), ())), preferred_element_type=jnp.float32
    )


def halves(value):
    high = value.astype(jnp.bfloat16)
    low = (value - high.astype(jnp.float32)).astype(jnp.bfloat16)
    return high, low


def wide(dot, left, right):
    left_high, left_low = halves(left)
    right_high, right_low = halves(right)
    return dot(left_high, right_high) + (dot(left_high, right_low) + dot(left_low, right_high))


def feature(value):
    return jnp.where(value > 0, value + 1.0, jnp.exp(jnp.minimum(value, 0.0)))


def feature_slope(value):
    return jnp.where(value > 0, 1.0, jnp.exp(jnp.minimum(value, 0.0)))


def key_value_project_kernel(tokens_ref, w_key_ref, w_value_ref, out_ref, row_ref):
    tokens = tokens_ref[...]
    head_dim = w_key_ref.shape[1]
    key = dot_nn(tokens, w_key_ref[...]).astype(jnp.bfloat16)
    value = dot_nn(tokens, w_value_ref[...]).astype(jnp.bfloat16)
    out_ref[:, :head_dim] = key
    out_ref[:, head_dim:] = value
    row_ref[:, :head_dim] = jnp.sum(feature(key.astype(jnp.float32)), axis=0, keepdims=True)
    row_ref[:, head_dim:] = jnp.mean(value.astype(jnp.float32), axis=0, keepdims=True)


def query_project_kernel(tokens_ref, w_query_ref, cot_ref, out_ref):
    head_dim = w_query_ref.shape[1]
    out_ref[:, :head_dim] = dot_nn(tokens_ref[...], w_query_ref[...]).astype(jnp.bfloat16)
    out_ref[:, head_dim:] = cot_ref[...]


def write_kernel(pair_ref, row_ref, memory_ref):
    head_dim = pair_ref.shape[1] // 2
    phi_key = feature(pair_ref[:, :head_dim].astype(jnp.float32))
    centred = pair_ref[:, head_dim:].astype(jnp.float32) - row_ref[:, head_dim:]
    memory_ref[0] = wide(dot_tn, phi_key, centred)


def grad_memory_kernel(pair_ref, rows_ref, mix_ref, out_ref):
    head_dim = pair_ref.shape[1] // 2
    phi_query = feature(pair_ref[:, :head_dim].astype(jnp.float32))
    norm = jnp.sum(rows_ref[:, :head_dim], axis=0, keepdims=True)
    denominator = jnp.sum(phi_query * norm, axis=1, keepdims=True) + 1.0
    grad_num = mix_ref[...] * pair_ref[:, head_dim:].astype(jnp.float32) / denominator
    out_ref[0] = wide(dot_tn, phi_query, grad_num)


def attend_kernel(
    has_prev_ref,
    query_ref,
    pair_ref,
    prev_ref,
    mix_ref,
    out_ref,
    grad_query_ref,
    stats_ref,
):
    seg_len, head_dim = pair_ref.shape[0], pair_ref.shape[1] // 2
    scale = head_dim ** (-0.5)
    query, cot = query_ref[:, :head_dim], query_ref[:, head_dim:]
    key, key_prev = pair_ref[:, :head_dim], prev_ref[:, :head_dim]
    value, value_prev = pair_ref[:, head_dim:], prev_ref[:, head_dim:]
    rows = lax.broadcasted_iota(jnp.int32, (seg_len, seg_len), 0)
    cols = lax.broadcasted_iota(jnp.int32, (seg_len, seg_len), 1)
    score_own = jnp.where(cols <= rows, dot_nt(query, key) * scale, -1e30)
    score_prev = jnp.where(has_prev_ref[0] > 0, dot_nt(query, key_prev) * scale, -1e30)
    row_max = jnp.maximum(
        jnp.max(score_own, axis=1, keepdims=True), jnp.max(score_prev, axis=1, keepdims=True)
    )
    weight_own = jnp.exp(score_own - row_max)
    weight_prev = jnp.exp(score_prev - row_max)
    inverse = 1.0 / (
        jnp.sum(weight_own, axis=1, keepdims=True) + jnp.sum(weight_prev, axis=1, keepdims=True)
    )
    soft_own = weight_own * inverse
    soft_prev = weight_prev * inverse
    out_ref[...] = dot_nn(soft_own.astype(jnp.bfloat16), value) + dot_nn(
        soft_prev.astype(jnp.bfloat16), value_prev
    )
    grad_local = ((1.0 - mix_ref[...]) * cot.astype(jnp.float32)).astype(jnp.bfloat16)
    grad_own = dot_nt(grad_local, value)
    grad_prev = dot_nt(grad_local, value_prev)
    row_dot = jnp.sum(soft_own * grad_own, axis=1, keepdims=True) + jnp.sum(
        soft_prev * grad_prev, axis=1, keepdims=True
    )
    score_grad_own = (soft_own * (grad_own - row_dot) * scale).astype(jnp.bfloat16)
    score_grad_prev = (soft_prev * (grad_prev - row_dot) * scale).astype(jnp.bfloat16)
    grad_query_ref[...] = dot_nn(score_grad_own, key) + dot_nn(score_grad_prev, key_prev)
    lane = lax.broadcasted_iota(jnp.int32, (seg_len, 128), 1)
    stats = jnp.where(
        lane == 0, row_max, jnp.where(lane == 1, inverse, jnp.where(lane == 2, row_dot, 0.0))
    )
    stats_ref[...] = jnp.transpose(stats)[:8]


def retrieve_kernel(
    query_ref,
    memory_ref,
    rows_ref,
    mix_ref,
    local_ref,
    grad_att_ref,
    blended_ref,
    grad_query_ref,
    grad_norm_ref,
):
    head_dim = query_ref.shape[1] // 2
    query = query_ref[:, :head_dim].astype(jnp.float32)
    phi_query = feature(query)
    norms = rows_ref[:, :head_dim]
    norm = jnp.sum(norms, axis=0, keepdims=True)
    memory = memory_ref[0].astype(jnp.float32) + wide(dot_tn, norms, rows_ref[:, head_dim:])
    mix = mix_ref[...]
    denominator = jnp.sum(phi_query * norm, axis=1, keepdims=True) + 1.0
    retrieved = wide(dot_nn, phi_query, memory) / denominator
    blended = mix * retrieved + (1.0 - mix) * local_ref[...]
    blended_ref[...] = blended.astype(jnp.bfloat16)
    grad_ret = mix * query_ref[:, head_dim:].astype(jnp.float32)
    grad_num = grad_ret / denominator
    grad_den = -jnp.sum(grad_ret * retrieved, axis=1, keepdims=True) / denominator
    grad_phi = wide(dot_nt, grad_num, memory) + grad_den * norm
    grad_norm_ref[...] = jnp.sum(grad_den * phi_query, axis=0, keepdims=True)
    grad_query = grad_att_ref[...] + grad_phi * feature_slope(query)
    grad_query_ref[...] = grad_query.astype(jnp.bfloat16)


def key_value_kernel(
    pair_ref,
    query_ref,
    stats_ref,
    query_next_ref,
    stats_next_ref,
    grad_memory_ref,
    mix_ref,
    grad_key_ref,
    grad_value_ref,
):
    seg_len, head_dim = pair_ref.shape[0], pair_ref.shape[1] // 2
    key, value = pair_ref[:, :head_dim], pair_ref[:, head_dim:]
    scale = head_dim ** (-0.5)
    keep = 1.0 - mix_ref[...]

    def part(query, cot, stats, causal):
        grad_local = (keep * cot.astype(jnp.float32)).astype(jnp.bfloat16)
        score = dot_nt(key, query) * scale
        if causal:
            rows = lax.broadcasted_iota(jnp.int32, score.shape, 0)
            cols = lax.broadcasted_iota(jnp.int32, score.shape, 1)
            score = jnp.where(rows <= cols, score, -1e30)
        soft = jnp.exp(score - stats[0:1]) * stats[1:2]
        grad_value = dot_nn(soft.astype(jnp.bfloat16), grad_local)
        grad_soft = dot_nt(value, grad_local)
        score_grad = (soft * (grad_soft - stats[2:3]) * scale).astype(jnp.bfloat16)
        return dot_nn(score_grad, query), grad_value

    def both(ref, stats, causal):
        return part(ref[:, :head_dim], ref[:, head_dim:], stats, causal)

    own_key, own_value = both(query_ref, stats_ref[...], True)
    next_key, next_value = both(query_next_ref, stats_next_ref[...], False)
    key_float = key.astype(jnp.float32)
    grad_memory = grad_memory_ref[0]
    phi_high, phi_low = halves(feature(key_float))
    from_memory = dot_nt(value, grad_memory)
    grad_key_ref[...] = own_key + next_key + from_memory * feature_slope(key_float)
    to_value = dot_nn(phi_high, grad_memory) + dot_nn(phi_low, grad_memory)
    grad_value_ref[...] = (own_value + next_value + to_value).astype(jnp.bfloat16)


def call(kernel, sizes, ins, outs):
    heads, seg_len, head_dim, model_dim, count = sizes
    blocks = {
        "t": (seg_len, model_dim),
        "w": (model_dim, head_dim),
        "c": (seg_len, head_dim),
        "p": (seg_len, 2 * head_dim),
        "r": (1, head_dim),
        "o": (1, 2 * head_dim),
        "R": (count, 2 * head_dim),
        "m": (1, head_dim, head_dim),
        "s": (8, seg_len),
    }

    def spec(kind):
        if kind == "f":
            return pl.BlockSpec(memory_space=pltpu.SMEM)
        if kind == "t":
            return pl.BlockSpec(blocks[kind], lambda h: (0, 0))
        if kind == "m":
            return pl.BlockSpec(blocks[kind], lambda h: (h, 0, 0))
        if kind == "s":
            return pl.BlockSpec(blocks[kind], lambda h: (h, 0))
        return pl.BlockSpec(blocks[kind], lambda h: (0, h))

    def shape(kind):
        block = blocks[kind]
        if kind in "ms":
            return (heads * block[0],) + block[1:]
        return (block[0], heads * block[1])

    return pl.pallas_call(
        kernel,
        grid=(heads,),
        in_specs=[spec(kind) for kind in ins],
        out_specs=[spec(kind) for kind, _ in outs],
        out_shape=[jax.ShapeDtypeStruct(shape(kind), dtype) for kind, dtype in outs],
        compiler_params=pltpu.CompilerParams(vmem_limit_bytes=VMEM_LIMIT),
        cost_estimate=pl.CostEstimate(flops=1000, bytes_accessed=1000, transcendentals=0),
    )


def local(inputs, w_query, w_key, w_value, gate_bias, cotangent):
    tokens = inputs[0]
    cot = cotangent[0]
    seg_len, model_dim = tokens.shape
    heads = gate_bias.shape[0]
    columns = w_query.shape[1]
    head_dim = columns // heads
    seq_count, seq_at = lax.axis_size("seq"), lax.axis_index("seq")
    dp_count, dp_at = lax.axis_size("dp"), lax.axis_index("dp")
    part_rows = model_dim // (seq_count * dp_count)
    f32, bf16 = jnp.float32, jnp.bfloat16

    def shifted(x, by, first=0, last=None):
        last = seq_count - 1 if last is None else last
        pairs = [
            (i, i + by) for i in range(first, last + 1) if 0 <= i + by < seq_count
        ]
        return lax.ppermute(x, "seq", pairs)

    def chain(own, by):
        total = jnp.zeros(own.shape, bf16)
        for hop in range(seq_count - 1):
            at = hop if by > 0 else seq_count - 1 - hop
            total = total + shifted((total + own).astype(bf16), by, at, at)
        return total

    def rows_before(own, by):
        window, step, known = own, 1, []
        while step < seq_count:
            arrived = shifted(window, by * step)
            known.append(arrived)
            window = jnp.concatenate([window, arrived], 0)
            step *= 2
        missing = -sum(part.shape[0] for part in known) % 8
        known.append(jnp.zeros((missing,) + own.shape[1:], own.dtype))
        return jnp.concatenate(known, 0)

    count = 1
    while count < seq_count:
        count *= 2
    count = -(-(count - 1) // 8) * 8
    sizes = (heads, seg_len, head_dim, model_dim, count)
    mix = jnp.repeat(jax.nn.sigmoid(gate_bias), head_dim)[None]
    has_prev = jnp.reshape((seq_at > 0).astype(jnp.int32), (1,))

    def rows_for(core):
        return jnp.concatenate(
            [
                lax.dynamic_slice_in_dim(tokens, (block * dp_count + core) * part_rows, part_rows, 1)
                for block in range(seq_count)
            ],
            1,
        )

    def from_core(x, step):
        return lax.ppermute(x, "dp", [(i, (i + step) % dp_count) for i in range(dp_count)])

    pair, row = call(key_value_project_kernel, sizes, "tww", (("p", bf16), ("o", f32)))(
        tokens, w_key, w_value
    )
    pair_prev = shifted(pair, 1)
    rows = rows_before(row, 1)
    (query,) = call(query_project_kernel, sizes, "twc", (("p", bf16),))(tokens, w_query, cot)
    query_next = shifted(query, -1)
    (memory_own,) = call(write_kernel, sizes, "po", (("m", f32),))(pair, row)
    memory = chain(memory_own, 1)
    (grad_memory_own,) = call(grad_memory_kernel, sizes, "pRr", (("m", f32),))(query, rows, mix)
    grad_memory = chain(grad_memory_own, -1)

    token_parts = [rows_for(dp_at)] + [
        from_core(rows_for((dp_at + step) % dp_count), step) for step in range(1, dp_count)
    ]

    local_out, grad_att, stats = call(
        attend_kernel, sizes, "fpppr", (("c", f32), ("c", f32), ("s", f32))
    )(has_prev, query, pair, pair_prev, mix)
    stats_next = shifted(stats, -1)
    blended, grad_query, grad_norm_own = call(
        retrieve_kernel, sizes, "pmRrcc", (("c", bf16), ("c", bf16), ("r", f32))
    )(query, memory, rows, mix, local_out, grad_att)
    grad_norm = jnp.sum(rows_before(grad_norm_own, -1), 0, keepdims=True)
    grad_key_rest, grad_value = call(
        key_value_kernel, sizes, "ppspsmr", (("c", f32), ("c", bf16))
    )(pair, query, stats, query_next, stats_next, grad_memory, mix)
    key = jnp.concatenate(
        [pair[:, 2 * h * head_dim : (2 * h + 1) * head_dim] for h in range(heads)], 1
    )
    grad_key = (grad_key_rest + grad_norm * feature_slope(key.astype(f32))).astype(bf16)

    contract = (((0,), (0,)), ((), ()))
    grad_scale = 1.0 / math.sqrt(seq_count * dp_count * seg_len)

    def weight_term(grad):
        grads = [grad] + [from_core(grad, step) for step in range(1, dp_count)]
        total = None
        for rows, term in zip(token_parts, grads):
            product = lax.dot_general(rows, term, contract, preferred_element_type=f32)
            total = product if total is None else total + product
        terms = total.reshape(seq_count, part_rows, columns)

        def block(index):
            return lax.dynamic_index_in_dim(terms, jnp.clip(index, 0, seq_count - 1), 0, False)

        ups = jnp.zeros((part_rows, columns), bf16)
        downs = ups
        for turn in range(1, seq_count):
            ahead = seq_count - turn
            ups = shifted(
                (ups.astype(f32) + block(seq_at + ahead)).astype(bf16), 1, 0, turn - 1
            )
            downs = shifted(
                (downs.astype(f32) + block(seq_at - ahead)).astype(bf16), -1, ahead
            )
        return (ups.astype(f32) + downs.astype(f32) + block(seq_at)) * grad_scale

    pieces = [weight_term(grad) for grad in (grad_query, grad_value, grad_key)]
    return (blended[None], jnp.stack([pieces[0], pieces[2], pieces[1]], 1))


def solution(mesh):
    return jax.shard_map(
        local,
        mesh=mesh,
        in_specs=(
            P("dp", "seq", None),
            P(None, "head"),
            P(None, "head"),
            P(None, "head"),
            P("head"),
            P("dp", "seq", "head"),
        ),
        out_specs=(P("dp", "seq", "head"), P(("seq", "dp"), None, "head")),
        check_vma=False,
    )
```

```python
import functools
import math

import jax
import jax.numpy as jnp
from jax import lax
from jax.experimental import pallas as pl
from jax.experimental.pallas import tpu as pltpu
from jax.sharding import PartitionSpec as P

VMEM_LIMIT = 48 * 1024 * 1024
SEQ, EVEN, CORE, PLACE = range(4)


def dot_nn(left, right):
    return lax.dot_general(
        left, right, (((1,), (0,)), ((), ())), preferred_element_type=jnp.float32
    )


def dot_nt(left, right):
    return lax.dot_general(
        left, right, (((1,), (1,)), ((), ())), preferred_element_type=jnp.float32
    )


def dot_tn(left, right):
    return lax.dot_general(
        left, right, (((0,), (0,)), ((), ())), preferred_element_type=jnp.float32
    )


def halves(value):
    high = value.astype(jnp.bfloat16)
    low = (value - high.astype(jnp.float32)).astype(jnp.bfloat16)
    return high, low


def wide(dot, left, right):
    left_high, left_low = halves(left)
    right_high, right_low = halves(right)
    return dot(left_high, right_high) + (dot(left_high, right_low) + dot(left_low, right_high))


def feature(value):
    return jnp.where(value > 0, value + 1.0, jnp.exp(jnp.minimum(value, 0.0)))


def feature_slope(value):
    return jnp.where(value > 0, 1.0, jnp.exp(jnp.minimum(value, 0.0)))


def copies_of(tokens_ref, tokens, weight_refs, weights, sems):
    pieces, depth = weights.shape[1:3]

    def token_copy(piece):
        at = pl.ds(piece * depth, depth)
        return pltpu.make_async_copy(tokens_ref.at[:, at], tokens.at[:, at], sems.at[piece])

    def weight_copy(which, piece):
        return pltpu.make_async_copy(
            weight_refs[which].at[pl.ds(piece * depth, depth)],
            weights.at[which, piece],
            sems.at[(which + 1) * pieces + piece],
        )

    for piece in range(pieces):
        token_copy(piece).start()
        weight_copy(0, piece).start()
    for which in range(1, len(weight_refs)):
        for piece in range(pieces):
            weight_copy(which, piece).start()

    def product(which):
        total = None
        for piece in range(pieces):
            if which == 0:
                token_copy(piece).wait()
            weight_copy(which, piece).wait()
            at = slice(piece * depth, (piece + 1) * depth)
            term = dot_nn(tokens[:, at], weights[which, piece])
            total = term if total is None else total + term
        return total.astype(jnp.bfloat16)

    return product


def project_kernel(
    heads,
    info_ref,
    tokens_ref,
    w_key_ref,
    w_value_ref,
    w_query_ref,
    cot_ref,
    pair_ref,
    query_ref,
    even_ref,
    odd_ref,
    row_ref,
    tokens,
    weights,
    cot,
    sems,
):
    product = copies_of(
        tokens_ref, tokens, (w_key_ref, w_value_ref, w_query_ref), weights, sems
    )
    cot_copy = pltpu.make_async_copy(cot_ref, cot, sems.at[sems.shape[0] - 1])
    cot_copy.start()
    head_dim = pair_ref.shape[1] // (2 * heads)
    even = info_ref[EVEN] > 0

    def put(ref, up, at, value):
        ref[:, at] = value

        @pl.when(even == up)
        def _():
            even_ref[:, at] = value

        @pl.when(even != up)
        def _():
            odd_ref[:, at] = value

    for which in range(2):
        result = product(which)
        for head in range(heads):
            part = result[:, head * head_dim : (head + 1) * head_dim]
            at = slice((2 * head + which) * head_dim, (2 * head + which + 1) * head_dim)
            put(pair_ref, True, at, part)
            wide_part = part.astype(jnp.float32)
            if which == 0:
                row_ref[:, at] = jnp.sum(feature(wide_part), axis=0, keepdims=True)
            else:
                row_ref[:, at] = jnp.mean(wide_part, axis=0, keepdims=True)
    query = product(2)
    cot_copy.wait()
    for head in range(heads):
        of_head = slice(head * head_dim, (head + 1) * head_dim)
        at = slice(2 * head * head_dim, (2 * head + 1) * head_dim)
        put(query_ref, False, at, query[:, of_head])
        at = slice((2 * head + 1) * head_dim, (2 * head + 2) * head_dim)
        put(query_ref, False, at, cot[:, of_head])


def lower_end(info_ref, route):
    distance, parity = route
    return lax.rem(lax.div(info_ref[SEQ], distance), 2) == parity


def total_from(info_ref, refs, routes, from_above):
    total = refs[0][0].astype(jnp.float32)
    for ref, route in zip(refs[1:], routes):
        wanted = lower_end(info_ref, route) == from_above
        total = total + jnp.where(wanted, ref[0].astype(jnp.float32), 0.0)
    return total


def neighbour_kernel(routes, info_ref, even_ref, odd_ref, far_ref, row_ref, mix_ref, *refs):
    prev_ref, next_ref, memory_ref, grad_memory_ref, row_prev_ref = refs[:5]
    even = info_ref[EVEN] > 0
    pair = jnp.where(even, odd_ref[...], even_ref[...])
    query = jnp.where(even, even_ref[...], odd_ref[...])
    prev_ref[...] = pair
    next_ref[...] = query
    head_dim = pair.shape[1] // 2
    phi_key = feature(pair[:, :head_dim].astype(jnp.float32))
    value = pair[:, head_dim:].astype(jnp.float32)
    mean = jnp.mean(value, axis=0, keepdims=True)
    centred = (value - mean).astype(jnp.bfloat16)
    memory = dot_tn(phi_key.astype(jnp.bfloat16), centred).astype(jnp.bfloat16)
    norm = jnp.sum(phi_key, axis=0, keepdims=True)
    norm = jnp.where(info_ref[SEQ] > 0, norm, 0.0)
    memory_ref[0] = memory
    row_prev_ref[:, :head_dim] = norm
    row_prev_ref[:, head_dim:] = mean

    phi_query = feature(query[:, :head_dim].astype(jnp.float32))
    norm = norm + jnp.sum(far_ref[:, :head_dim], axis=0, keepdims=True) + row_ref[:, :head_dim]
    denominator = jnp.sum(phi_query * norm, axis=1, keepdims=True) + 1.0
    grad_num = mix_ref[...] * query[:, head_dim:].astype(jnp.float32) / denominator
    grad_memory = dot_tn(phi_query.astype(jnp.bfloat16), grad_num.astype(jnp.bfloat16))
    grad_memory = grad_memory.astype(jnp.bfloat16)
    grad_memory_ref[0] = grad_memory
    for ref, route in zip(refs[5:], routes):
        ref[0] = jnp.where(lower_end(info_ref, route), memory, grad_memory)


def attend_kernel(
    info_ref,
    query_ref,
    pair_ref,
    prev_ref,
    mix_ref,
    out_ref,
    grad_query_ref,
    stats_ref,
):
    seg_len, head_dim = pair_ref.shape[0], pair_ref.shape[1] // 2
    scale = head_dim ** (-0.5)
    query, cot = query_ref[:, :head_dim], query_ref[:, head_dim:]
    key, key_prev = pair_ref[:, :head_dim], prev_ref[:, :head_dim]
    value, value_prev = pair_ref[:, head_dim:], prev_ref[:, head_dim:]
    rows = lax.broadcasted_iota(jnp.int32, (seg_len, seg_len), 0)
    cols = lax.broadcasted_iota(jnp.int32, (seg_len, seg_len), 1)
    score_own = jnp.where(cols <= rows, dot_nt(query, key) * scale, -1e30)
    score_prev = jnp.where(info_ref[SEQ] > 0, dot_nt(query, key_prev) * scale, -1e30)
    row_max = jnp.maximum(
        jnp.max(score_own, axis=1, keepdims=True), jnp.max(score_prev, axis=1, keepdims=True)
    )
    weight_own = jnp.exp(score_own - row_max)
    weight_prev = jnp.exp(score_prev - row_max)
    inverse = 1.0 / (
        jnp.sum(weight_own, axis=1, keepdims=True) + jnp.sum(weight_prev, axis=1, keepdims=True)
    )
    soft_own = weight_own * inverse
    soft_prev = weight_prev * inverse
    out_ref[...] = dot_nn(soft_own.astype(jnp.bfloat16), value) + dot_nn(
        soft_prev.astype(jnp.bfloat16), value_prev
    )
    grad_local = ((1.0 - mix_ref[...]) * cot.astype(jnp.float32)).astype(jnp.bfloat16)
    grad_own = dot_nt(grad_local, value)
    grad_prev = dot_nt(grad_local, value_prev)
    row_dot = jnp.sum(soft_own * grad_own, axis=1, keepdims=True) + jnp.sum(
        soft_prev * grad_prev, axis=1, keepdims=True
    )
    score_grad_own = (soft_own * (grad_own - row_dot) * scale).astype(jnp.bfloat16)
    score_grad_prev = (soft_prev * (grad_prev - row_dot) * scale).astype(jnp.bfloat16)
    grad_query_ref[...] = dot_nn(score_grad_own, key) + dot_nn(score_grad_prev, key_prev)
    lane = lax.broadcasted_iota(jnp.int32, (seg_len, 128), 1)
    stats = jnp.where(
        lane == 0, row_max, jnp.where(lane == 1, inverse, jnp.where(lane == 2, row_dot, 0.0))
    )
    stats_ref[...] = jnp.transpose(stats)[:8]


def retrieve_kernel(
    routes, info_ref, query_ref, row_prev_ref, far_ref, mix_ref, local_ref, grad_att_ref, stats_ref, *refs
):
    blended_ref, grad_query_ref, note_ref = refs[-3:]
    head_dim = query_ref.shape[1] // 2
    query = query_ref[:, :head_dim].astype(jnp.float32)
    phi_query = feature(query)
    free = lax.broadcasted_iota(jnp.int32, far_ref.shape, 0) == 0
    rows = jnp.where(free, row_prev_ref[...], far_ref[...])
    norms = rows[:, :head_dim]
    norm = jnp.sum(norms, axis=0, keepdims=True)
    memory = total_from(info_ref, refs[:-3], routes, False) + wide(dot_tn, norms, rows[:, head_dim:])
    mix = mix_ref[...]
    denominator = jnp.sum(phi_query * norm, axis=1, keepdims=True) + 1.0
    retrieved = wide(dot_nn, phi_query, memory) / denominator
    blended = mix * retrieved + (1.0 - mix) * local_ref[...]
    blended_ref[...] = blended.astype(jnp.bfloat16)
    grad_ret = mix * query_ref[:, head_dim:].astype(jnp.float32)
    grad_num = grad_ret / denominator
    grad_den = -jnp.sum(grad_ret * retrieved, axis=1, keepdims=True) / denominator
    grad_phi = wide(dot_nt, grad_num, memory) + grad_den * norm
    seg_len = query.shape[0]
    note_ref[:8] = stats_ref[...]
    grad_norm = jnp.sum(grad_den * phi_query, axis=0, keepdims=True)
    if seg_len > head_dim:
        filler = jnp.zeros((1, seg_len - head_dim), jnp.float32)
        grad_norm = jnp.concatenate([grad_norm, filler], 1)
    note_ref[8:] = jnp.broadcast_to(grad_norm, (8, grad_norm.shape[1]))
    grad_query = grad_att_ref[...] + grad_phi * feature_slope(query)
    grad_query_ref[...] = grad_query.astype(jnp.bfloat16)


def key_value_kernel(
    routes, notes, info_ref, pair_ref, query_ref, note_ref, query_next_ref, mix_ref, *refs
):
    note_refs, grad_key_ref, grad_value_ref = refs[:notes], refs[-2], refs[-1]
    note_next_ref = note_refs[0]
    seg_len, head_dim = pair_ref.shape[0], pair_ref.shape[1] // 2
    key, value = pair_ref[:, :head_dim], pair_ref[:, head_dim:]
    scale = head_dim ** (-0.5)
    keep = 1.0 - mix_ref[...]

    def part(query, cot, stats, causal):
        grad_local = (keep * cot.astype(jnp.float32)).astype(jnp.bfloat16)
        score = dot_nt(key, query) * scale
        if causal:
            rows = lax.broadcasted_iota(jnp.int32, score.shape, 0)
            cols = lax.broadcasted_iota(jnp.int32, score.shape, 1)
            score = jnp.where(rows <= cols, score, -1e30)
        soft = jnp.exp(score - stats[0:1]) * stats[1:2]
        grad_value = dot_nn(soft.astype(jnp.bfloat16), grad_local)
        grad_soft = dot_nt(value, grad_local)
        score_grad = (soft * (grad_soft - stats[2:3]) * scale).astype(jnp.bfloat16)
        return dot_nn(score_grad, query), grad_value

    def both(ref, stats, causal):
        return part(ref[:, :head_dim], ref[:, head_dim:], stats, causal)

    own_key, own_value = both(query_ref, note_ref[:8], True)
    next_key, next_value = both(query_next_ref, note_next_ref[:8], False)
    key_float = key.astype(jnp.float32)
    grad_memory = total_from(info_ref, refs[notes:-2], routes, True).astype(jnp.bfloat16)
    phi_high, phi_low = halves(feature(key_float))
    from_memory = dot_nt(value, grad_memory)
    norm = note_next_ref[8:9, :head_dim]
    for ref in note_refs[1:]:
        norm = norm + ref[8:9, :head_dim]
    from_memory = (from_memory + norm) * feature_slope(key_float)
    grad_key_ref[...] = (own_key + next_key + from_memory).astype(jnp.bfloat16)
    to_value = dot_nn(phi_high, grad_memory) + dot_nn(phi_low, grad_memory)
    grad_value_ref[...] = (own_value + next_value + to_value).astype(jnp.bfloat16)


def pack_kernel(seq_count, dp_count, info_ref, *refs):
    for tokens_ref, out_ref in zip(refs[:dp_count], refs[dp_count:]):
        part_rows = out_ref.shape[0] // seq_count
        own_rows = dp_count * part_rows
        for block in range(seq_count):
            at = pl.multiple_of(info_ref[CORE] * part_rows + block * own_rows, 128)
            out_ref[block * part_rows : (block + 1) * part_rows] = jnp.transpose(
                tokens_ref[:, pl.ds(at, part_rows)]
            )


def row_blocks_kernel(info_ref, *refs):
    *refs, out_ref, first_ref = refs
    count = len(refs) // 2
    total = dot_nn(refs[0][...], refs[count][...])
    for rows, grad in zip(refs[1:count], refs[count + 1 :]):
        total = total + dot_nn(rows[...], grad[...])
    total = total.astype(jnp.bfloat16)
    out_ref[0] = total
    block = pl.program_id(0)
    last = pl.num_programs(0) - 1
    place = jnp.where(info_ref[SEQ] == 0, last - block, block)

    @pl.when(place < 2)
    def _():
        first_ref[place] = total


def inner_kernel(arrived_ref, far_ref, near_ref, far_out_ref, near_out_ref):
    for at, (ref, out_ref) in enumerate(((far_ref, far_out_ref), (near_ref, near_out_ref))):
        total = arrived_ref[at].astype(jnp.float32) + ref[0].astype(jnp.float32)
        out_ref[...] = total.astype(jnp.bfloat16)


def outer_kernel(info_ref, arrived_ref, terms_ref, out_ref):
    term = terms_ref[0].astype(jnp.float32)
    total = term + arrived_ref[...].astype(jnp.float32)
    out_ref[...] = total.astype(jnp.bfloat16)


def finish_kernel(scale, info_ref, even_ref, odd_ref, terms_ref, *refs):
    out_ref = refs[-1]
    total = even_ref[...].astype(jnp.float32) + odd_ref[...].astype(jnp.float32)
    out_ref[0] = (total + terms_ref[0].astype(jnp.float32)) * scale


def limits(vmem=VMEM_LIMIT, **more):
    return dict(
        compiler_params=pltpu.CompilerParams(vmem_limit_bytes=vmem),
        cost_estimate=pl.CostEstimate(flops=0, bytes_accessed=0, transcendentals=0),
        **more,
    )


SMEM_SPEC = pl.BlockSpec(memory_space=pltpu.SMEM)
HBM_SPEC = pl.BlockSpec(memory_space=pltpu.HBM)
VMEM_SPEC = pl.BlockSpec(memory_space=pltpu.VMEM)


def call(kernel, sizes, ins, outs):
    heads, seg_len, head_dim, count = sizes
    blocks = {
        "c": (seg_len, head_dim),
        "p": (seg_len, 2 * head_dim),
        "r": (1, head_dim),
        "o": (1, 2 * head_dim),
        "R": (count, 2 * head_dim),
        "m": (1, head_dim, head_dim),
        "s": (8, seg_len),
        "n": (16, max(seg_len, head_dim)),
    }

    def spec(kind):
        if kind == "f":
            return SMEM_SPEC
        if kind == "m":
            return pl.BlockSpec(blocks[kind], lambda h: (h, 0, 0))
        if kind in "sn":
            return pl.BlockSpec(blocks[kind], lambda h: (h, 0))
        return pl.BlockSpec(blocks[kind], lambda h: (0, h))

    def shape(kind):
        block = blocks[kind]
        if kind in "msn":
            return (heads * block[0],) + block[1:]
        return (block[0], heads * block[1])

    return pl.pallas_call(
        kernel,
        grid=(heads,),
        in_specs=[spec(kind) for kind in ins],
        out_specs=[spec(kind) for kind, _ in outs],
        out_shape=[jax.ShapeDtypeStruct(shape(kind), dtype) for kind, dtype in outs],
        **limits(),
    )


def local(inputs, w_query, w_key, w_value, gate_bias, cotangent):
    tokens = inputs[0]
    cot = cotangent[0]
    seg_len, model_dim = tokens.shape
    heads = gate_bias.shape[0]
    columns = w_query.shape[1]
    head_dim = columns // heads
    seq_count, seq_at = lax.axis_size("seq"), lax.axis_index("seq")
    dp_count, dp_at = lax.axis_size("dp"), lax.axis_index("dp")
    plane, place = lax.axis_size("head"), lax.axis_index("head")
    part_rows = model_dim // (seq_count * dp_count)
    f32, bf16 = jnp.float32, jnp.bfloat16
    info = jnp.stack([seq_at, 1 - seq_at % 2, dp_at, place]).astype(jnp.int32)

    def shifted(x, by, first=0, last=None):
        last = seq_count - 1 if last is None else last
        pairs = [
            (i, i + by) for i in range(first, last + 1) if 0 <= i + by < seq_count
        ]
        return lax.ppermute(x, "seq", pairs)

    def swapped(x, distance, parity, lowest=0):
        pairs = []
        for i in range(seq_count - distance):
            if (i // distance) % 2 == parity:
                if i >= lowest:
                    pairs.append((i, i + distance))
                if seq_count - 1 - (i + distance) >= lowest:
                    pairs.append((i + distance, i))
        return lax.ppermute(x, "seq", pairs) if pairs else None

    def from_core(x, step):
        return lax.ppermute(x, "dp", [(i, (i + step) % dp_count) for i in range(dp_count)])

    count = -(-(seq_count - 1) // 8) * 8
    sizes = (heads, seg_len, head_dim, count)
    mix = jnp.repeat(jax.nn.sigmoid(gate_bias), head_dim)[None]

    by_swaps = seq_count == 4 and part_rows % 128 == 0
    pieces = 2
    wide_shape = jax.ShapeDtypeStruct((seg_len, 2 * columns), bf16)
    pair, query, even_message, odd_message, row = pl.pallas_call(
        functools.partial(project_kernel, heads),
        in_specs=[SMEM_SPEC] + [HBM_SPEC] * 5,
        out_specs=[VMEM_SPEC] * 5,
        out_shape=[wide_shape] * 4 + [jax.ShapeDtypeStruct((1, 2 * columns), f32)],
        scratch_shapes=[
            pltpu.VMEM((seg_len, model_dim), bf16),
            pltpu.VMEM((3, pieces, model_dim // pieces, columns), bf16),
            pltpu.VMEM((seg_len, columns), bf16),
            pltpu.SemaphoreType.DMA((4 * pieces + 1,)),
        ],
        **limits(62 * 1024 * 1024),
    )(info, tokens, w_key, w_value, w_query, cot)
    even_arrived = swapped(even_message, 1, 0)
    odd_arrived = swapped(odd_message, 1, 1)
    far_rows = [shifted(row, step) for step in range(2, seq_count)]
    free = jnp.zeros_like(row)
    pad = jnp.zeros((count - seq_count + 1, 2 * columns), f32)
    near = jnp.concatenate([free] + far_rows[:-1] + [free, pad], 0)
    far = jnp.concatenate([free] + far_rows + [pad], 0)

    routes = [
        (distance, parity)
        for distance in range(1, seq_count - 1)
        for parity in range(2)
        if any(
            (i // distance) % 2 == parity and (i > 0 or i + distance < seq_count - 1)
            for i in range(seq_count - distance)
        )
    ]
    routes = [route for route in routes if route != (1, 0)] + [(1, 0)]
    over = "m" * len(routes)
    pair_prev, query_next, memory, grad_memory, row_prev, *sent = call(
        functools.partial(neighbour_kernel, routes),
        sizes,
        "fppRor",
        [("p", bf16)] * 2 + [("m", bf16)] * 2 + [("o", f32)] + [("m", bf16)] * len(routes),
    )(info, even_arrived, odd_arrived, near, row, mix)
    arrived = [swapped(part, *route, lowest=1) for part, route in zip(sent, routes)]
    local_out, grad_att, stats = call(
        attend_kernel, sizes, "fpppr", (("c", f32), ("c", f32), ("s", f32))
    )(info, query, pair, pair_prev, mix)
    if by_swaps:
        all_tokens = [tokens] + [from_core(tokens, step) for step in range(1, dp_count)]
        all_tokens, stats = lax.optimization_barrier((all_tokens, stats))
        token_parts = pl.pallas_call(
            functools.partial(pack_kernel, seq_count, dp_count),
            in_specs=[SMEM_SPEC] + [VMEM_SPEC] * dp_count,
            out_specs=[VMEM_SPEC] * dp_count,
            out_shape=[jax.ShapeDtypeStruct((seq_count * part_rows, seg_len), bf16)] * dp_count,
            **limits(),
        )(info, *all_tokens)
        local_out, token_parts = lax.optimization_barrier((local_out, token_parts))
    blended, grad_query, note = call(
        functools.partial(retrieve_kernel, routes),
        sizes,
        "fpoRrccsm" + over,
        (("c", bf16), ("c", bf16), ("n", f32)),
    )(info, query, row_prev, far, mix, local_out, grad_att, stats, memory, *arrived)
    notes = [shifted(note, -step) for step in range(1, seq_count)]

    def row_blocks(grad):
        grads = [grad] + [from_core(grad, step) for step in range(1, dp_count)]
        return pl.pallas_call(
            row_blocks_kernel,
            grid=(seq_count,),
            in_specs=[SMEM_SPEC]
            + [pl.BlockSpec((part_rows, seg_len), lambda b: (b, 0))] * dp_count
            + [pl.BlockSpec((seg_len, columns), lambda b: (0, 0))] * dp_count,
            out_specs=[
                pl.BlockSpec((1, part_rows, columns), lambda b: (b, 0, 0)),
                pl.BlockSpec((2, part_rows, columns), lambda b: (0, 0, 0)),
            ],
            out_shape=[
                jax.ShapeDtypeStruct((seq_count, part_rows, columns), bf16),
                jax.ShapeDtypeStruct((2, part_rows, columns), bf16),
            ],
            **limits(),
        )(info, *token_parts, *grads)

    grad_scale = 1.0 / math.sqrt(seq_count * dp_count * seg_len)
    block = (part_rows, columns)
    part_shape = jax.ShapeDtypeStruct(block, bf16)
    whole = pl.BlockSpec(block, lambda i, info: (0, 0))

    def on_terms(kernel, ins, outs, out_shape, **more):
        return pl.pallas_call(
            kernel,
            grid_spec=pltpu.PrefetchScalarGridSpec(
                num_scalar_prefetch=1, grid=(1,), in_specs=ins, out_specs=outs
            ),
            out_shape=out_shape,
            **limits(**more),
        )

    def at_block(index):
        return pl.BlockSpec((1,) + block, lambda i, info: (index(info[SEQ]), 0, 0))

    def swapped_ends(first):
        last = seq_count - 1
        return lax.ppermute(first, "seq", [(0, 1), (last, last - 1)])

    def inner_messages(terms, arrived):
        def inner(info_ref, *refs):
            inner_kernel(*refs)

        return on_terms(
            inner,
            [
                pl.BlockSpec((2,) + block, lambda i, info: (0, 0, 0)),
                at_block(lambda z: jnp.where(z < 2, 3, 0)),
                at_block(lambda z: jnp.where(z < 2, 2, 1)),
            ],
            [whole, whole],
            [part_shape] * 2,
        )(info, arrived, terms, terms)

    def over_middle(terms, arrived):
        return [swapped(message, 1, 1) for message in inner_messages(terms, arrived)]

    def end_message(terms, far):
        return on_terms(
            outer_kernel,
            [whole, at_block(lambda z: lax.bitwise_xor(z, 1))],
            whole,
            part_shape,
        )(info, far, terms)

    def to_ends(terms, far):
        return swapped(end_message(terms, far), 1, 0)

    def finish(terms, even, odd, which, into=()):
        return on_terms(
            functools.partial(finish_kernel, grad_scale),
            [whole, whole, at_block(lambda z: z)] + [HBM_SPEC] * len(into),
            pl.BlockSpec((1,) + block, lambda i, info: (which, 0, 0)),
            jax.ShapeDtypeStruct((3,) + block, f32),
            input_output_aliases={4: 0} if into else {},
        )(info, even, odd, terms, *into)

    if by_swaps:
        query_terms, query_first = row_blocks(grad_query)
        notes[0], query_terms, query_first = lax.optimization_barrier(
            (notes[0], query_terms, query_first)
        )
        query_ends = swapped_ends(query_first)
    grad_key, grad_value = call(
        functools.partial(key_value_kernel, routes, len(notes)),
        sizes,
        "fppnpr" + "n" * len(notes) + over + "m",
        (("c", bf16), ("c", bf16)),
    )(info, pair, query, note, query_next, mix, *notes, grad_memory, *arrived)
    if not by_swaps:
        contract = (((0,), (0,)), ((), ()))

        def rows_for(core):
            return jnp.concatenate(
                [
                    lax.dynamic_slice_in_dim(
                        tokens, (block * dp_count + core) * part_rows, part_rows, 1
                    )
                    for block in range(seq_count)
                ],
                1,
            )

        token_columns = [rows_for(dp_at)] + [
            from_core(rows_for((dp_at + step) % dp_count), step) for step in range(1, dp_count)
        ]

        def summed(grad):
            grads = [grad] + [from_core(grad, step) for step in range(1, dp_count)]
            terms = sum(
                lax.dot_general(part, term, contract, preferred_element_type=f32)
                for part, term in zip(token_columns, grads)
            ).reshape(seq_count, part_rows, grad.shape[1])

            def block(index):
                index = jnp.clip(index, 0, seq_count - 1)
                return lax.dynamic_index_in_dim(terms, index, 0, False)

            ups = downs = jnp.zeros((part_rows, grad.shape[1]), bf16)
            for turn in range(1, seq_count):
                ahead = seq_count - turn
                ups = shifted((ups + block(seq_at + ahead)).astype(bf16), 1, 0, turn - 1)
                downs = shifted((downs + block(seq_at - ahead)).astype(bf16), -1, ahead)
            return ups + downs + block(seq_at)

        rows = summed(jnp.concatenate([grad_query, grad_key, grad_value], 1)) * grad_scale
        return (blended[None], rows.reshape(part_rows, 3, columns))

    value_terms, value_first = row_blocks(grad_value)
    value_ends = swapped_ends(value_first)
    grad_key, value_terms = lax.optimization_barrier((grad_key, value_terms))
    key_terms, key_first = row_blocks(grad_key)
    key_ends = swapped_ends(key_first)
    key_terms, query_ends = lax.optimization_barrier((key_terms, query_ends))
    query_far, query_near = over_middle(query_terms, query_ends)
    value_ends, query_far, query_near = lax.optimization_barrier(
        (value_ends, query_far, query_near)
    )
    query_even = to_ends(query_terms, query_far)
    value_far, value_near = over_middle(value_terms, value_ends)
    key_ends, value_far, value_near = lax.optimization_barrier((key_ends, value_far, value_near))
    value_even = to_ends(value_terms, value_far)
    key_far, key_near = over_middle(key_terms, key_ends)
    key_far, query_even = lax.optimization_barrier((key_far, query_even))
    key_even = to_ends(key_terms, key_far)
    grad_weights = finish(query_terms, query_even, query_near, 0)
    grad_weights = finish(value_terms, value_even, value_near, 2, (grad_weights,))
    grad_weights = finish(key_terms, key_even, key_near, 1, (grad_weights,))
    return (blended[None], jnp.transpose(grad_weights, (1, 0, 2)))


def solution(mesh):
    return jax.shard_map(
        local,
        mesh=mesh,
        in_specs=(
            P("dp", "seq", None),
            P(None, "head"),
            P(None, "head"),
            P(None, "head"),
            P("head"),
            P("dp", "seq", "head"),
        ),
        out_specs=(P("dp", "seq", "head"), P(("seq", "dp"), None, "head")),
        check_vma=False,
    )
```

```python
import functools
import math

import jax
import jax.numpy as jnp
from jax import lax
from jax.experimental import pallas as pl
from jax.experimental.pallas import tpu as pltpu
from jax.sharding import PartitionSpec as P

VMEM_LIMIT = 32 * 1024 * 1024
SEQ, EVEN, CORE, PLACE = range(4)


def dot_nn(left, right):
    return lax.dot_general(
        left, right, (((1,), (0,)), ((), ())), preferred_element_type=jnp.float32
    )


def dot_nt(left, right):
    return lax.dot_general(
        left, right, (((1,), (1,)), ((), ())), preferred_element_type=jnp.float32
    )


def dot_tn(left, right):
    return lax.dot_general(
        left, right, (((0,), (0,)), ((), ())), preferred_element_type=jnp.float32
    )


def halves(value):
    high = value.astype(jnp.bfloat16)
    low = (value - high.astype(jnp.float32)).astype(jnp.bfloat16)
    return high, low


def wide(dot, left, right):
    left_high, left_low = halves(left)
    right_high, right_low = halves(right)
    return dot(left_high, right_high) + (dot(left_high, right_low) + dot(left_low, right_high))


def feature(value):
    return jnp.where(value > 0, value + 1.0, jnp.exp(jnp.minimum(value, 0.0)))


def feature_slope(value):
    return jnp.where(value > 0, 1.0, jnp.exp(jnp.minimum(value, 0.0)))


def copies_of(tokens_ref, tokens, weight_refs, weights, sems):
    pieces, depth = weights.shape[1:3]

    def token_copy(piece):
        at = pl.ds(piece * depth, depth)
        return pltpu.make_async_copy(tokens_ref.at[:, at], tokens.at[:, at], sems.at[piece])

    def weight_copy(which, piece):
        return pltpu.make_async_copy(
            weight_refs[which].at[pl.ds(piece * depth, depth)],
            weights.at[which, piece],
            sems.at[(which + 1) * pieces + piece],
        )

    for piece in range(pieces):
        token_copy(piece).start()
        weight_copy(0, piece).start()
    for which in range(1, len(weight_refs)):
        for piece in range(pieces):
            weight_copy(which, piece).start()

    def product(which):
        total = None
        for piece in range(pieces):
            if which == 0:
                token_copy(piece).wait()
            weight_copy(which, piece).wait()
            at = slice(piece * depth, (piece + 1) * depth)
            term = dot_nn(tokens[:, at], weights[which, piece])
            total = term if total is None else total + term
        return total.astype(jnp.bfloat16)

    return product


def project_kernel(
    heads,
    info_ref,
    tokens_ref,
    w_key_ref,
    w_value_ref,
    w_query_ref,
    cot_ref,
    pair_ref,
    query_ref,
    even_ref,
    odd_ref,
    row_ref,
    tokens,
    weights,
    cot,
    sems,
):
    product = copies_of(
        tokens_ref, tokens, (w_key_ref, w_value_ref, w_query_ref), weights, sems
    )
    cot_copy = pltpu.make_async_copy(cot_ref, cot, sems.at[sems.shape[0] - 1])
    cot_copy.start()
    head_dim = pair_ref.shape[1] // (2 * heads)
    even = info_ref[EVEN] > 0

    def put(ref, up, at, value):
        ref[:, at] = value

        @pl.when(even == up)
        def _():
            even_ref[:, at] = value

        @pl.when(even != up)
        def _():
            odd_ref[:, at] = value

    for which in range(2):
        result = product(which)
        for head in range(heads):
            part = result[:, head * head_dim : (head + 1) * head_dim]
            at = slice((2 * head + which) * head_dim, (2 * head + which + 1) * head_dim)
            put(pair_ref, True, at, part)
            wide_part = part.astype(jnp.float32)
            if which == 0:
                row_ref[:, at] = jnp.sum(feature(wide_part), axis=0, keepdims=True)
            else:
                row_ref[:, at] = jnp.mean(wide_part, axis=0, keepdims=True)
    query = product(2)
    cot_copy.wait()
    for head in range(heads):
        of_head = slice(head * head_dim, (head + 1) * head_dim)
        at = slice(2 * head * head_dim, (2 * head + 1) * head_dim)
        put(query_ref, False, at, query[:, of_head])
        at = slice((2 * head + 1) * head_dim, (2 * head + 2) * head_dim)
        put(query_ref, False, at, cot[:, of_head])


def lower_end(info_ref, route):
    distance, parity = route
    return lax.rem(lax.div(info_ref[SEQ], distance), 2) == parity


def total_from(info_ref, refs, routes, from_above):
    total = refs[0][0].astype(jnp.float32)
    for ref, route in zip(refs[1:], routes):
        wanted = lower_end(info_ref, route) == from_above
        total = total + jnp.where(wanted, ref[0].astype(jnp.float32), 0.0)
    return total


def neighbour_kernel(routes, info_ref, even_ref, odd_ref, far_ref, row_ref, mix_ref, *refs):
    prev_ref, next_ref, memory_ref, grad_memory_ref, row_prev_ref = refs[:5]
    even = info_ref[EVEN] > 0
    pair = jnp.where(even, odd_ref[...], even_ref[...])
    query = jnp.where(even, even_ref[...], odd_ref[...])
    prev_ref[...] = pair
    next_ref[...] = query
    head_dim = pair.shape[1] // 2
    phi_key = feature(pair[:, :head_dim].astype(jnp.float32))
    value = pair[:, head_dim:].astype(jnp.float32)
    mean = jnp.mean(value, axis=0, keepdims=True)
    centred = (value - mean).astype(jnp.bfloat16)
    memory = dot_tn(phi_key.astype(jnp.bfloat16), centred).astype(jnp.bfloat16)
    norm = jnp.sum(phi_key, axis=0, keepdims=True)
    norm = jnp.where(info_ref[SEQ] > 0, norm, 0.0)
    memory_ref[0] = memory
    row_prev_ref[:, :head_dim] = norm
    row_prev_ref[:, head_dim:] = mean

    phi_query = feature(query[:, :head_dim].astype(jnp.float32))
    norm = norm + jnp.sum(far_ref[:, :head_dim], axis=0, keepdims=True) + row_ref[:, :head_dim]
    denominator = jnp.sum(phi_query * norm, axis=1, keepdims=True) + 1.0
    grad_num = mix_ref[...] * query[:, head_dim:].astype(jnp.float32) / denominator
    grad_memory = dot_tn(phi_query.astype(jnp.bfloat16), grad_num.astype(jnp.bfloat16))
    grad_memory = grad_memory.astype(jnp.bfloat16)
    grad_memory_ref[0] = grad_memory
    for ref, route in zip(refs[5:], routes):
        ref[0] = jnp.where(lower_end(info_ref, route), memory, grad_memory)


def attend_kernel(
    info_ref,
    query_ref,
    pair_ref,
    prev_ref,
    mix_ref,
    out_ref,
    grad_query_ref,
    stats_ref,
):
    seg_len, head_dim = pair_ref.shape[0], pair_ref.shape[1] // 2
    scale = head_dim ** (-0.5)
    query, cot = query_ref[:, :head_dim], query_ref[:, head_dim:]
    key, key_prev = pair_ref[:, :head_dim], prev_ref[:, :head_dim]
    value, value_prev = pair_ref[:, head_dim:], prev_ref[:, head_dim:]
    rows = lax.broadcasted_iota(jnp.int32, (seg_len, seg_len), 0)
    cols = lax.broadcasted_iota(jnp.int32, (seg_len, seg_len), 1)
    score_own = jnp.where(cols <= rows, dot_nt(query, key) * scale, -1e30)
    score_prev = jnp.where(info_ref[SEQ] > 0, dot_nt(query, key_prev) * scale, -1e30)
    row_max = jnp.maximum(
        jnp.max(score_own, axis=1, keepdims=True), jnp.max(score_prev, axis=1, keepdims=True)
    )
    weight_own = jnp.exp(score_own - row_max)
    weight_prev = jnp.exp(score_prev - row_max)
    inverse = 1.0 / (
        jnp.sum(weight_own, axis=1, keepdims=True) + jnp.sum(weight_prev, axis=1, keepdims=True)
    )
    soft_own = weight_own * inverse
    soft_prev = weight_prev * inverse
    out_ref[...] = dot_nn(soft_own.astype(jnp.bfloat16), value) + dot_nn(
        soft_prev.astype(jnp.bfloat16), value_prev
    )
    grad_local = ((1.0 - mix_ref[...]) * cot.astype(jnp.float32)).astype(jnp.bfloat16)
    grad_own = dot_nt(grad_local, value)
    grad_prev = dot_nt(grad_local, value_prev)
    row_dot = jnp.sum(soft_own * grad_own, axis=1, keepdims=True) + jnp.sum(
        soft_prev * grad_prev, axis=1, keepdims=True
    )
    score_grad_own = (soft_own * (grad_own - row_dot) * scale).astype(jnp.bfloat16)
    score_grad_prev = (soft_prev * (grad_prev - row_dot) * scale).astype(jnp.bfloat16)
    grad_query_ref[...] = dot_nn(score_grad_own, key) + dot_nn(score_grad_prev, key_prev)
    lane = lax.broadcasted_iota(jnp.int32, (seg_len, 128), 1)
    stats = jnp.where(
        lane == 0, row_max, jnp.where(lane == 1, inverse, jnp.where(lane == 2, row_dot, 0.0))
    )
    stats_ref[...] = jnp.transpose(stats)[:8]


def retrieve_kernel(
    routes, info_ref, query_ref, row_prev_ref, far_ref, mix_ref, local_ref, grad_att_ref, stats_ref, *refs
):
    blended_ref, grad_query_ref, note_ref = refs[-3:]
    head_dim = query_ref.shape[1] // 2
    query = query_ref[:, :head_dim].astype(jnp.float32)
    phi_query = feature(query)
    free = lax.broadcasted_iota(jnp.int32, far_ref.shape, 0) == 0
    rows = jnp.where(free, row_prev_ref[...], far_ref[...])
    norms = rows[:, :head_dim]
    norm = jnp.sum(norms, axis=0, keepdims=True)
    memory = total_from(info_ref, refs[:-3], routes, False) + wide(dot_tn, norms, rows[:, head_dim:])
    mix = mix_ref[...]
    denominator = jnp.sum(phi_query * norm, axis=1, keepdims=True) + 1.0
    retrieved = wide(dot_nn, phi_query, memory) / denominator
    blended = mix * retrieved + (1.0 - mix) * local_ref[...]
    blended_ref[...] = blended.astype(jnp.bfloat16)
    grad_ret = mix * query_ref[:, head_dim:].astype(jnp.float32)
    grad_num = grad_ret / denominator
    grad_den = -jnp.sum(grad_ret * retrieved, axis=1, keepdims=True) / denominator
    grad_phi = wide(dot_nt, grad_num, memory) + grad_den * norm
    seg_len = query.shape[0]
    note_ref[:8] = stats_ref[...]
    grad_norm = jnp.sum(grad_den * phi_query, axis=0, keepdims=True)
    if seg_len > head_dim:
        filler = jnp.zeros((1, seg_len - head_dim), jnp.float32)
        grad_norm = jnp.concatenate([grad_norm, filler], 1)
    note_ref[8:] = jnp.broadcast_to(grad_norm, (8, grad_norm.shape[1]))
    grad_query = grad_att_ref[...] + grad_phi * feature_slope(query)
    grad_query_ref[...] = grad_query.astype(jnp.bfloat16)


def key_value_kernel(
    routes, notes, orders, info_ref, pair_ref, query_ref, note_ref, query_next_ref, mix_ref, *refs
):
    note_refs, grad_key_ref, grad_value_ref = refs[:notes], refs[-2], refs[-1]
    stats_next = note_refs[0][:8]
    seg_len, head_dim = pair_ref.shape[0], pair_ref.shape[1] // 2
    key, value = pair_ref[:, :head_dim], pair_ref[:, head_dim:]
    scale = head_dim ** (-0.5)
    keep = 1.0 - mix_ref[...]

    def part(query, cot, stats, causal):
        grad_local = (keep * cot.astype(jnp.float32)).astype(jnp.bfloat16)
        score = dot_nt(key, query) * scale
        if causal:
            rows = lax.broadcasted_iota(jnp.int32, score.shape, 0)
            cols = lax.broadcasted_iota(jnp.int32, score.shape, 1)
            score = jnp.where(rows <= cols, score, -1e30)
        soft = jnp.exp(score - stats[0:1]) * stats[1:2]
        grad_value = dot_nn(soft.astype(jnp.bfloat16), grad_local)
        grad_soft = dot_nt(value, grad_local)
        score_grad = (soft * (grad_soft - stats[2:3]) * scale).astype(jnp.bfloat16)
        return dot_nn(score_grad, query), grad_value

    def both(ref, stats, causal):
        return part(ref[:, :head_dim], ref[:, head_dim:], stats, causal)

    own_key, own_value = both(query_ref, note_ref[:8], True)
    next_key, next_value = both(query_next_ref, stats_next, False)
    key_float = key.astype(jnp.float32)
    grad_memory = total_from(info_ref, refs[notes : len(refs) - 2 - orders], routes, True).astype(jnp.bfloat16)
    phi_high, phi_low = halves(feature(key_float))
    from_memory = dot_nt(value, grad_memory)
    norm = note_refs[0][8:9, :head_dim]
    for ref in note_refs[1:]:
        norm = norm + ref[8:9, :head_dim]
    from_memory = (from_memory + norm) * feature_slope(key_float)
    grad_key_ref[...] = (own_key + next_key + from_memory).astype(jnp.bfloat16)
    to_value = dot_nn(phi_high, grad_memory) + dot_nn(phi_low, grad_memory)
    grad_value_ref[...] = (own_value + next_value + to_value).astype(jnp.bfloat16)


def pack_kernel(seq_count, dp_count, info_ref, *refs):
    for tokens_ref, out_ref in zip(refs[:dp_count], refs[dp_count:]):
        part_rows = out_ref.shape[0] // seq_count
        own_rows = dp_count * part_rows
        for block in range(seq_count):
            at = pl.multiple_of(info_ref[CORE] * part_rows + block * own_rows, 128)
            out_ref[block * part_rows : (block + 1) * part_rows] = jnp.transpose(
                tokens_ref[:, pl.ds(at, part_rows)]
            )


def row_blocks_kernel(info_ref, *refs):
    *refs, out_ref, first_ref = refs
    count = len(refs) // 2
    total = dot_nn(refs[0][...], refs[count][...])
    for rows, grad in zip(refs[1:count], refs[count + 1 :]):
        total = total + dot_nn(rows[...], grad[...])
    total = total.astype(jnp.bfloat16)
    out_ref[0] = total
    block = pl.program_id(0)
    last = pl.num_programs(0) - 1
    place = jnp.where(info_ref[SEQ] == 0, last - block, block)

    @pl.when(place < 2)
    def _():
        first_ref[place] = total


def inner_kernel(arrived_ref, far_ref, near_ref, *out_refs):
    for at, ref in enumerate((far_ref, near_ref)):
        total = arrived_ref[at].astype(jnp.float32) + ref[0].astype(jnp.float32)
        out_ref = out_refs[at] if len(out_refs) > 1 else out_refs[0]
        out_ref[at if len(out_refs) == 1 else 0] = total.astype(jnp.bfloat16)


def outer_kernel(info_ref, arrived_ref, terms_ref, *refs):
    term = terms_ref[0].astype(jnp.float32)
    total = term + arrived_ref[0].astype(jnp.float32)
    refs[-1][...] = total.astype(jnp.bfloat16)


def finish_kernel(scale, info_ref, even_ref, odd_ref, terms_ref, *refs):
    out_ref = refs[-1]
    total = even_ref[...].astype(jnp.float32) + odd_ref[0].astype(jnp.float32)
    out_ref[0] = (total + terms_ref[0].astype(jnp.float32)) * scale


def limits(vmem=VMEM_LIMIT, **more):
    return dict(
        compiler_params=pltpu.CompilerParams(vmem_limit_bytes=vmem),
        cost_estimate=pl.CostEstimate(flops=0, bytes_accessed=0, transcendentals=0),
        **more,
    )


SMEM_SPEC = pl.BlockSpec(memory_space=pltpu.SMEM)
HBM_SPEC = pl.BlockSpec(memory_space=pltpu.HBM)
VMEM_SPEC = pl.BlockSpec(memory_space=pltpu.VMEM)


def call(kernel, sizes, ins, outs):
    heads, seg_len, head_dim, count = sizes
    blocks = {
        "c": (seg_len, head_dim),
        "p": (seg_len, 2 * head_dim),
        "r": (1, head_dim),
        "o": (1, 2 * head_dim),
        "R": (count, 2 * head_dim),
        "m": (1, head_dim, head_dim),
        "s": (8, seg_len),
        "n": (16, max(seg_len, head_dim)),
    }

    def spec(kind):
        if kind == "f":
            return SMEM_SPEC
        if kind == "x":
            return HBM_SPEC
        if kind == "m":
            return pl.BlockSpec(blocks[kind], lambda h: (h, 0, 0))
        if kind in "sn":
            return pl.BlockSpec(blocks[kind], lambda h: (h, 0))
        return pl.BlockSpec(blocks[kind], lambda h: (0, h))

    def shape(kind):
        block = blocks[kind]
        if kind in "msn":
            return (heads * block[0],) + block[1:]
        return (block[0], heads * block[1])

    return pl.pallas_call(
        kernel,
        grid=(heads,),
        in_specs=[spec(kind) for kind in ins],
        out_specs=[spec(kind) for kind, _ in outs],
        out_shape=[jax.ShapeDtypeStruct(shape(kind), dtype) for kind, dtype in outs],
        **limits(),
    )


def local(inputs, w_query, w_key, w_value, gate_bias, cotangent):
    tokens = inputs[0]
    cot = cotangent[0]
    seg_len, model_dim = tokens.shape
    heads = gate_bias.shape[0]
    columns = w_query.shape[1]
    head_dim = columns // heads
    seq_count, seq_at = lax.axis_size("seq"), lax.axis_index("seq")
    dp_count, dp_at = lax.axis_size("dp"), lax.axis_index("dp")
    plane, place = lax.axis_size("head"), lax.axis_index("head")
    part_rows = model_dim // (seq_count * dp_count)
    f32, bf16 = jnp.float32, jnp.bfloat16
    info = jnp.stack([seq_at, 1 - seq_at % 2, dp_at, place]).astype(jnp.int32)

    def shifted(x, by, first=0, last=None):
        last = seq_count - 1 if last is None else last
        pairs = [
            (i, i + by) for i in range(first, last + 1) if 0 <= i + by < seq_count
        ]
        return lax.ppermute(x, "seq", pairs)

    def swapped(x, distance, parity, lowest=0):
        pairs = []
        for i in range(seq_count - distance):
            if (i // distance) % 2 == parity:
                if i >= lowest:
                    pairs.append((i, i + distance))
                if seq_count - 1 - (i + distance) >= lowest:
                    pairs.append((i + distance, i))
        return lax.ppermute(x, "seq", pairs) if pairs else None

    def nudge(x):
        return from_core(x.reshape(-1, x.shape[-1])[:16, :128], 1)

    def from_core(x, step):
        return lax.ppermute(x, "dp", [(i, (i + step) % dp_count) for i in range(dp_count)])

    count = -(-(seq_count - 1) // 8) * 8
    sizes = (heads, seg_len, head_dim, count)
    mix = jnp.repeat(jax.nn.sigmoid(gate_bias), head_dim)[None]

    by_swaps = seq_count == 4 and part_rows % 128 == 0
    pieces = 2
    wide_shape = jax.ShapeDtypeStruct((seg_len, 2 * columns), bf16)
    pair, query, even_message, odd_message, row = pl.pallas_call(
        functools.partial(project_kernel, heads),
        in_specs=[SMEM_SPEC] + [HBM_SPEC] * 5,
        out_specs=[VMEM_SPEC] * 5,
        out_shape=[wide_shape] * 4 + [jax.ShapeDtypeStruct((1, 2 * columns), f32)],
        scratch_shapes=[
            pltpu.VMEM((seg_len, model_dim), bf16),
            pltpu.VMEM((3, pieces, model_dim // pieces, columns), bf16),
            pltpu.VMEM((seg_len, columns), bf16),
            pltpu.SemaphoreType.DMA((4 * pieces + 1,)),
        ],
        **limits(48 * 1024 * 1024),
    )(info, tokens, w_key, w_value, w_query, cot)
    even_arrived = swapped(even_message, 1, 0)
    odd_arrived = swapped(odd_message, 1, 1)
    far_rows = [shifted(row, step) for step in range(2, seq_count)]
    free = jnp.zeros_like(row)
    pad = jnp.zeros((count - seq_count + 1, 2 * columns), f32)
    near = jnp.concatenate([free] + far_rows[:-1] + [free, pad], 0)
    far = jnp.concatenate([free] + far_rows + [pad], 0)

    routes = [
        (distance, parity)
        for distance in range(1, seq_count - 1)
        for parity in range(2)
        if any(
            (i // distance) % 2 == parity and (i > 0 or i + distance < seq_count - 1)
            for i in range(seq_count - distance)
        )
    ]
    routes = [route for route in routes if route != (1, 0)] + [(1, 0)]
    over = "m" * len(routes)
    pair_prev, query_next, memory, grad_memory, row_prev, *sent = call(
        functools.partial(neighbour_kernel, routes),
        sizes,
        "fppRor",
        [("p", bf16)] * 2 + [("m", bf16)] * 2 + [("o", f32)] + [("m", bf16)] * len(routes),
    )(info, even_arrived, odd_arrived, near, row, mix)
    arrived = [swapped(part, *route, lowest=1) for part, route in zip(sent, routes)]
    local_out, grad_att, stats = call(
        attend_kernel, sizes, "fpppr", (("c", f32), ("c", f32), ("s", f32))
    )(info, query, pair, pair_prev, mix)
    if by_swaps:
        all_tokens = [tokens] + [from_core(tokens, step) for step in range(1, dp_count)]
        all_tokens, stats = lax.optimization_barrier((all_tokens, stats))
        token_parts = pl.pallas_call(
            functools.partial(pack_kernel, seq_count, dp_count),
            in_specs=[SMEM_SPEC] + [VMEM_SPEC] * dp_count,
            out_specs=[VMEM_SPEC] * dp_count,
            out_shape=[jax.ShapeDtypeStruct((seq_count * part_rows, seg_len), bf16)] * dp_count,
            **limits(),
        )(info, *all_tokens)
        local_out, token_parts = lax.optimization_barrier((local_out, token_parts))
    blended, grad_query, note = call(
        functools.partial(retrieve_kernel, routes),
        sizes,
        "fpoRrccsm" + over,
        (("c", bf16), ("c", bf16), ("n", f32)),
    )(info, query, row_prev, far, mix, local_out, grad_att, stats, memory, *arrived)
    notes = [shifted(note, -step) for step in range(1, seq_count)]

    def of_cores(grad):
        return [grad] + [from_core(grad, step) for step in range(1, dp_count)]

    def row_blocks(grads):
        return pl.pallas_call(
            row_blocks_kernel,
            grid=(seq_count,),
            in_specs=[SMEM_SPEC]
            + [pl.BlockSpec((part_rows, seg_len), lambda b: (b, 0))] * dp_count
            + [pl.BlockSpec((seg_len, columns), lambda b: (0, 0))] * dp_count,
            out_specs=[
                pl.BlockSpec((1, part_rows, columns), lambda b: (b, 0, 0)),
                pl.BlockSpec((2, part_rows, columns), lambda b: (0, 0, 0)),
            ],
            out_shape=[
                jax.ShapeDtypeStruct((seq_count, part_rows, columns), bf16),
                jax.ShapeDtypeStruct((2, part_rows, columns), bf16),
            ],
            **limits(),
        )(info, *token_parts, *grads)

    grad_scale = 1.0 / math.sqrt(seq_count * dp_count * seg_len)
    block = (part_rows, columns)
    part_shape = jax.ShapeDtypeStruct(block, bf16)
    whole = pl.BlockSpec(block, lambda i, info: (0, 0))
    first = pl.BlockSpec((1,) + block, lambda i, info: (0, 0, 0))

    def on_terms(kernel, ins, outs, out_shape, **more):
        return pl.pallas_call(
            kernel,
            grid_spec=pltpu.PrefetchScalarGridSpec(
                num_scalar_prefetch=1, grid=(1,), in_specs=ins, out_specs=outs
            ),
            out_shape=out_shape,
            **limits(**more),
        )

    def at_block(index):
        return pl.BlockSpec((1,) + block, lambda i, info: (index(info[SEQ]), 0, 0))

    def swapped_ends(first):
        last = seq_count - 1
        return lax.ppermute(first, "seq", [(0, 1), (last, last - 1)])

    def inner_messages(terms, arrived, arrays, *order):
        def inner(info_ref, *refs):
            inner_kernel(*refs[:3], *refs[-arrays:])

        size = (2 // arrays,) + block
        return on_terms(
            inner,
            [
                pl.BlockSpec((2,) + block, lambda i, info: (0, 0, 0)),
                at_block(lambda z: jnp.where(z < 2, 3, 0)),
                at_block(lambda z: jnp.where(z < 2, 2, 1)),
            ]
            + [HBM_SPEC] * len(order),
            [pl.BlockSpec(size, lambda i, info: (0, 0, 0))] * arrays,
            [jax.ShapeDtypeStruct(size, bf16)] * arrays,
        )(info, arrived, terms, terms, *order)

    def end_message(terms, far, *order):
        return on_terms(
            outer_kernel,
            [first, at_block(lambda z: lax.bitwise_xor(z, 1))] + [HBM_SPEC] * len(order),
            whole,
            part_shape,
        )(info, far, terms, *order)

    def finish(terms, even, odd, which, into=()):
        last = odd.shape[0] - 1
        odd_block = pl.BlockSpec((1,) + block, lambda i, info: (last, 0, 0))
        return on_terms(
            functools.partial(finish_kernel, grad_scale),
            [whole, odd_block, at_block(lambda z: z)] + [HBM_SPEC] * len(into),
            pl.BlockSpec((1,) + block, lambda i, info: (which, 0, 0)),
            jax.ShapeDtypeStruct((3,) + block, f32),
            input_output_aliases={4: 0} if into else {},
        )(info, even, odd, terms, *into)

    if by_swaps:
        query_terms, query_first = row_blocks(of_cores(grad_query))
        notes[0], query_terms, query_first = lax.optimization_barrier(
            (notes[0], query_terms, query_first)
        )
        query_ends = swapped_ends(query_first)
        order = [nudge(query_first)]
    else:
        order = []
    grad_key, grad_value = call(
        functools.partial(key_value_kernel, routes, len(notes), len(order)),
        sizes,
        "fppnpr" + "n" * len(notes) + over + "m" + "x" * len(order),
        (("c", bf16), ("c", bf16)),
    )(info, pair, query, note, query_next, mix, *notes, grad_memory, *arrived, *order)
    if not by_swaps:
        contract = (((0,), (0,)), ((), ()))

        def rows_for(core):
            return jnp.concatenate(
                [
                    lax.dynamic_slice_in_dim(
                        tokens, (block * dp_count + core) * part_rows, part_rows, 1
                    )
                    for block in range(seq_count)
                ],
                1,
            )

        token_columns = [rows_for(dp_at)] + [
            from_core(rows_for((dp_at + step) % dp_count), step) for step in range(1, dp_count)
        ]

        def summed(grad):
            grads = [grad] + [from_core(grad, step) for step in range(1, dp_count)]
            terms = sum(
                lax.dot_general(part, term, contract, preferred_element_type=f32)
                for part, term in zip(token_columns, grads)
            ).reshape(seq_count, part_rows, grad.shape[1])

            def block(index):
                index = jnp.clip(index, 0, seq_count - 1)
                return lax.dynamic_index_in_dim(terms, index, 0, False)

            ups = downs = jnp.zeros((part_rows, grad.shape[1]), bf16)
            for turn in range(1, seq_count):
                ahead = seq_count - turn
                ups = shifted((ups + block(seq_at + ahead)).astype(bf16), 1, 0, turn - 1)
                downs = shifted((downs + block(seq_at - ahead)).astype(bf16), -1, ahead)
            return ups + downs + block(seq_at)

        rows = summed(jnp.concatenate([grad_query, grad_key, grad_value], 1)) * grad_scale
        return (blended[None], rows.reshape(part_rows, 3, columns))

    values, keys = lax.optimization_barrier((of_cores(grad_value), of_cores(grad_key)))
    value_terms, value_first = row_blocks(values)
    value_ends = swapped_ends(value_first)
    keys, value_terms = lax.optimization_barrier((keys, value_terms))
    key_terms, key_first = row_blocks(keys)
    key_ends = swapped_ends(key_first)

    (message,) = inner_messages(query_terms, query_ends, 1, key_terms)
    query_odd = swapped(message, 1, 1)
    (message,) = inner_messages(value_terms, value_ends, 1, message)
    value_odd = swapped(message, 1, 1)
    message = end_message(query_terms, query_odd, message)
    query_even = swapped(message, 1, 0)
    messages = inner_messages(key_terms, key_ends, 2, message)
    key_far, key_near = [swapped(message, 1, 1) for message in messages]
    message = end_message(value_terms, value_odd, query_even, *messages)
    value_even = swapped(message, 1, 0)
    message = end_message(key_terms, key_far, message)
    key_even = swapped(message, 1, 0)
    grad_weights = finish(query_terms, query_even, query_odd, 0)
    grad_weights = finish(value_terms, value_even, value_odd, 2, (grad_weights,))
    grad_weights = finish(key_terms, key_even, key_near, 1, (grad_weights,))
    return (blended[None], jnp.transpose(grad_weights, (1, 0, 2)))


def solution(mesh):
    return jax.shard_map(
        local,
        mesh=mesh,
        in_specs=(
            P("dp", "seq", None),
            P(None, "head"),
            P(None, "head"),
            P(None, "head"),
            P("head"),
            P("dp", "seq", "head"),
        ),
        out_specs=(P("dp", "seq", "head"), P(("seq", "dp"), None, "head")),
        check_vma=False,
    )
```

```python
import functools
import math

import jax
import jax.numpy as jnp
from jax import lax
from jax.experimental import pallas as pl
from jax.experimental.pallas import tpu as pltpu
from jax.sharding import PartitionSpec as P

VMEM_LIMIT = 32 * 1024 * 1024
SEQ, EVEN, CORE, PLACE = range(4)


def dot_nn(left, right):
    return lax.dot_general(
        left, right, (((1,), (0,)), ((), ())), preferred_element_type=jnp.float32
    )


def dot_nt(left, right):
    return lax.dot_general(
        left, right, (((1,), (1,)), ((), ())), preferred_element_type=jnp.float32
    )


def dot_tn(left, right):
    return lax.dot_general(
        left, right, (((0,), (0,)), ((), ())), preferred_element_type=jnp.float32
    )


def halves(value):
    high = value.astype(jnp.bfloat16)
    low = (value - high.astype(jnp.float32)).astype(jnp.bfloat16)
    return high, low


def wide(dot, left, right):
    left_high, left_low = halves(left)
    right_high, right_low = halves(right)
    return dot(left_high, right_high) + (dot(left_high, right_low) + dot(left_low, right_high))


def feature(value):
    return jnp.where(value > 0, value + 1.0, jnp.exp(jnp.minimum(value, 0.0)))


def feature_slope(value):
    return jnp.where(value > 0, 1.0, jnp.exp(jnp.minimum(value, 0.0)))


def copies_of(tokens_ref, tokens, weight_refs, weights, sems):
    pieces, depth = weights.shape[1:3]

    def token_copy(piece):
        at = pl.ds(piece * depth, depth)
        return pltpu.make_async_copy(tokens_ref.at[:, at], tokens.at[:, at], sems.at[piece])

    def weight_copy(which, piece):
        return pltpu.make_async_copy(
            weight_refs[which].at[pl.ds(piece * depth, depth)],
            weights.at[which, piece],
            sems.at[(which + 1) * pieces + piece],
        )

    for piece in range(pieces):
        token_copy(piece).start()
        weight_copy(0, piece).start()
    for which in range(1, len(weight_refs)):
        for piece in range(pieces):
            weight_copy(which, piece).start()

    def product(which):
        for piece in range(pieces):
            if which == 0:
                token_copy(piece).wait()
            weight_copy(which, piece).wait()
        parts = []
        half = weights.shape[3] // 2
        for columns in (slice(0, half), slice(half, 2 * half)):
            total = None
            for piece in range(pieces):
                at = slice(piece * depth, (piece + 1) * depth)
                term = dot_nn(tokens[:, at], weights[which, piece, :, columns])
                total = term if total is None else total + term
            parts.append(total.astype(jnp.bfloat16))
        return jnp.concatenate(parts, 1)

    return product


def project_kernel(
    heads,
    info_ref,
    tokens_ref,
    w_key_ref,
    w_value_ref,
    w_query_ref,
    cot_ref,
    pair_ref,
    query_ref,
    even_ref,
    odd_ref,
    row_ref,
    tokens,
    weights,
    cot,
    sems,
):
    product = copies_of(
        tokens_ref, tokens, (w_key_ref, w_value_ref, w_query_ref), weights, sems
    )
    cot_copy = pltpu.make_async_copy(cot_ref, cot, sems.at[sems.shape[0] - 1])
    cot_copy.start()
    head_dim = pair_ref.shape[1] // (2 * heads)
    even = info_ref[EVEN] > 0

    def put(ref, up, at, value):
        ref[:, at] = value

        @pl.when(even == up)
        def _():
            even_ref[:, at] = value

        @pl.when(even != up)
        def _():
            odd_ref[:, at] = value

    for which in range(2):
        result = product(which)
        for head in range(heads):
            part = result[:, head * head_dim : (head + 1) * head_dim]
            at = slice((2 * head + which) * head_dim, (2 * head + which + 1) * head_dim)
            put(pair_ref, True, at, part)
            wide_part = part.astype(jnp.float32)
            if which == 0:
                row_ref[:, at] = jnp.sum(feature(wide_part), axis=0, keepdims=True)
            else:
                row_ref[:, at] = jnp.mean(wide_part, axis=0, keepdims=True)
    query = product(2)
    cot_copy.wait()
    for head in range(heads):
        of_head = slice(head * head_dim, (head + 1) * head_dim)
        at = slice(2 * head * head_dim, (2 * head + 1) * head_dim)
        put(query_ref, False, at, query[:, of_head])
        at = slice((2 * head + 1) * head_dim, (2 * head + 2) * head_dim)
        put(query_ref, False, at, cot[:, of_head])


def lower_end(info_ref, route):
    distance, parity = route
    return lax.rem(lax.div(info_ref[SEQ], distance), 2) == parity


def total_from(info_ref, refs, routes, from_above):
    total = refs[0][0].astype(jnp.float32)
    for ref, route in zip(refs[1:], routes):
        wanted = lower_end(info_ref, route) == from_above
        total = total + jnp.where(wanted, ref[0].astype(jnp.float32), 0.0)
    return total


def neighbour_kernel(routes, info_ref, even_ref, odd_ref, far_ref, row_ref, mix_ref, *refs):
    prev_ref, next_ref, memory_ref, grad_memory_ref, row_prev_ref = refs[:5]
    even = info_ref[EVEN] > 0
    pair = jnp.where(even, odd_ref[...], even_ref[...])
    query = jnp.where(even, even_ref[...], odd_ref[...])
    prev_ref[...] = pair
    next_ref[...] = query
    head_dim = pair.shape[1] // 2
    phi_key = feature(pair[:, :head_dim].astype(jnp.float32))
    value = pair[:, head_dim:].astype(jnp.float32)
    mean = jnp.mean(value, axis=0, keepdims=True)
    centred = (value - mean).astype(jnp.bfloat16)
    memory = dot_tn(phi_key.astype(jnp.bfloat16), centred).astype(jnp.bfloat16)
    norm = jnp.sum(phi_key, axis=0, keepdims=True)
    norm = jnp.where(info_ref[SEQ] > 0, norm, 0.0)
    memory_ref[0] = memory
    row_prev_ref[:, :head_dim] = norm
    row_prev_ref[:, head_dim:] = mean

    phi_query = feature(query[:, :head_dim].astype(jnp.float32))
    norm = norm + jnp.sum(far_ref[:, :head_dim], axis=0, keepdims=True) + row_ref[:, :head_dim]
    denominator = jnp.sum(phi_query * norm, axis=1, keepdims=True) + 1.0
    grad_num = mix_ref[...] * query[:, head_dim:].astype(jnp.float32) / denominator
    grad_memory = dot_tn(phi_query.astype(jnp.bfloat16), grad_num.astype(jnp.bfloat16))
    grad_memory = grad_memory.astype(jnp.bfloat16)
    grad_memory_ref[0] = grad_memory
    for ref, route in zip(refs[5:], routes):
        ref[0] = jnp.where(lower_end(info_ref, route), memory, grad_memory)


def attend_kernel(
    info_ref,
    query_ref,
    pair_ref,
    prev_ref,
    mix_ref,
    out_ref,
    grad_query_ref,
    stats_ref,
):
    seg_len, head_dim = pair_ref.shape[0], pair_ref.shape[1] // 2
    scale = head_dim ** (-0.5)
    query, cot = query_ref[:, :head_dim], query_ref[:, head_dim:]
    key, key_prev = pair_ref[:, :head_dim], prev_ref[:, :head_dim]
    value, value_prev = pair_ref[:, head_dim:], prev_ref[:, head_dim:]
    rows = lax.broadcasted_iota(jnp.int32, (seg_len, seg_len), 0)
    cols = lax.broadcasted_iota(jnp.int32, (seg_len, seg_len), 1)
    score_own = jnp.where(cols <= rows, dot_nt(query, key) * scale, -1e30)
    score_prev = jnp.where(info_ref[SEQ] > 0, dot_nt(query, key_prev) * scale, -1e30)
    row_max = jnp.maximum(
        jnp.max(score_own, axis=1, keepdims=True), jnp.max(score_prev, axis=1, keepdims=True)
    )
    weight_own = jnp.exp(score_own - row_max)
    weight_prev = jnp.exp(score_prev - row_max)
    inverse = 1.0 / (
        jnp.sum(weight_own, axis=1, keepdims=True) + jnp.sum(weight_prev, axis=1, keepdims=True)
    )
    soft_own = weight_own * inverse
    soft_prev = weight_prev * inverse
    out_ref[...] = dot_nn(soft_own.astype(jnp.bfloat16), value) + dot_nn(
        soft_prev.astype(jnp.bfloat16), value_prev
    )
    grad_local = ((1.0 - mix_ref[...]) * cot.astype(jnp.float32)).astype(jnp.bfloat16)
    grad_own = dot_nt(grad_local, value)
    grad_prev = dot_nt(grad_local, value_prev)
    row_dot = jnp.sum(soft_own * grad_own, axis=1, keepdims=True) + jnp.sum(
        soft_prev * grad_prev, axis=1, keepdims=True
    )
    score_grad_own = (soft_own * (grad_own - row_dot) * scale).astype(jnp.bfloat16)
    score_grad_prev = (soft_prev * (grad_prev - row_dot) * scale).astype(jnp.bfloat16)
    grad_query_ref[...] = dot_nn(score_grad_own, key) + dot_nn(score_grad_prev, key_prev)
    lane = lax.broadcasted_iota(jnp.int32, (seg_len, 128), 1)
    stats = jnp.where(
        lane == 0, row_max, jnp.where(lane == 1, inverse, jnp.where(lane == 2, row_dot, 0.0))
    )
    stats_ref[...] = jnp.transpose(stats)[:8]


def retrieve_kernel(
    routes, info_ref, query_ref, row_prev_ref, far_ref, mix_ref, local_ref, grad_att_ref, stats_ref, *refs
):
    blended_ref, grad_query_ref, note_ref = refs[-3:]
    head_dim = query_ref.shape[1] // 2
    query = query_ref[:, :head_dim].astype(jnp.float32)
    phi_query = feature(query)
    free = lax.broadcasted_iota(jnp.int32, far_ref.shape, 0) == 0
    rows = jnp.where(free, row_prev_ref[...], far_ref[...])
    norms = rows[:, :head_dim]
    norm = jnp.sum(norms, axis=0, keepdims=True)
    memory = total_from(info_ref, refs[:-3], routes, False) + wide(dot_tn, norms, rows[:, head_dim:])
    mix = mix_ref[...]
    denominator = jnp.sum(phi_query * norm, axis=1, keepdims=True) + 1.0
    retrieved = wide(dot_nn, phi_query, memory) / denominator
    blended = mix * retrieved + (1.0 - mix) * local_ref[...]
    blended_ref[...] = blended.astype(jnp.bfloat16)
    grad_ret = mix * query_ref[:, head_dim:].astype(jnp.float32)
    grad_num = grad_ret / denominator
    grad_den = -jnp.sum(grad_ret * retrieved, axis=1, keepdims=True) / denominator
    grad_phi = wide(dot_nt, grad_num, memory) + grad_den * norm
    seg_len = query.shape[0]
    note_ref[:8] = stats_ref[...]
    grad_norm = jnp.sum(grad_den * phi_query, axis=0, keepdims=True)
    if seg_len > head_dim:
        filler = jnp.zeros((1, seg_len - head_dim), jnp.float32)
        grad_norm = jnp.concatenate([grad_norm, filler], 1)
    note_ref[8:] = jnp.broadcast_to(grad_norm, (8, grad_norm.shape[1]))
    grad_query = grad_att_ref[...] + grad_phi * feature_slope(query)
    grad_query_ref[...] = grad_query.astype(jnp.bfloat16)


def key_value_kernel(
    routes, notes, info_ref, pair_ref, query_ref, note_ref, query_next_ref, mix_ref, *refs
):
    note_refs, grad_key_ref, grad_value_ref = refs[:notes], refs[-2], refs[-1]
    stats_next = note_refs[0][:8]
    seg_len, head_dim = pair_ref.shape[0], pair_ref.shape[1] // 2
    key, value = pair_ref[:, :head_dim], pair_ref[:, head_dim:]
    scale = head_dim ** (-0.5)
    keep = 1.0 - mix_ref[...]

    def part(query, cot, stats, causal):
        grad_local = (keep * cot.astype(jnp.float32)).astype(jnp.bfloat16)
        score = dot_nt(key, query) * scale
        if causal:
            rows = lax.broadcasted_iota(jnp.int32, score.shape, 0)
            cols = lax.broadcasted_iota(jnp.int32, score.shape, 1)
            score = jnp.where(rows <= cols, score, -1e30)
        soft = jnp.exp(score - stats[0:1]) * stats[1:2]
        grad_value = dot_nn(soft.astype(jnp.bfloat16), grad_local)
        grad_soft = dot_nt(value, grad_local)
        score_grad = (soft * (grad_soft - stats[2:3]) * scale).astype(jnp.bfloat16)
        return dot_nn(score_grad, query), grad_value

    def both(ref, stats, causal):
        return part(ref[:, :head_dim], ref[:, head_dim:], stats, causal)

    own_key, own_value = both(query_ref, note_ref[:8], True)
    next_key, next_value = both(query_next_ref, stats_next, False)
    key_float = key.astype(jnp.float32)
    grad_memory = total_from(info_ref, refs[notes:-2], routes, True).astype(jnp.bfloat16)
    phi_high, phi_low = halves(feature(key_float))
    from_memory = dot_nt(value, grad_memory)
    norm = note_refs[0][8:9, :head_dim]
    for ref in note_refs[1:]:
        norm = norm + ref[8:9, :head_dim]
    from_memory = (from_memory + norm) * feature_slope(key_float)
    grad_key_ref[...] = (own_key + next_key + from_memory).astype(jnp.bfloat16)
    to_value = dot_nn(phi_high, grad_memory) + dot_nn(phi_low, grad_memory)
    grad_value_ref[...] = (own_value + next_value + to_value).astype(jnp.bfloat16)


def pack_kernel(seq_count, dp_count, info_ref, *refs):
    for tokens_ref, out_ref in zip(refs[:dp_count], refs[dp_count:]):
        part_rows = out_ref.shape[0] // seq_count
        own_rows = dp_count * part_rows
        for block in range(seq_count):
            at = pl.multiple_of(info_ref[CORE] * part_rows + block * own_rows, 128)
            out_ref[block * part_rows : (block + 1) * part_rows] = jnp.transpose(
                tokens_ref[:, pl.ds(at, part_rows)]
            )


def row_blocks_kernel(info_ref, *refs):
    *refs, out_ref, first_ref = refs
    count = len(refs) // 2
    blocks, part_rows = out_ref.shape[:2]
    for block in range(blocks):
        rows = slice(block * part_rows, (block + 1) * part_rows)
        total = dot_nn(refs[0][rows], refs[count][...])
        for columns, grad in zip(refs[1:count], refs[count + 1 :]):
            total = total + dot_nn(columns[rows], grad[...])
        total = total.astype(jnp.bfloat16)
        out_ref[block] = total
        place = jnp.where(info_ref[SEQ] == 0, blocks - 1 - block, block)

        @pl.when(place < 2)
        def _(place=place, total=total):
            first_ref[place] = total


def inner_kernel(arrived_ref, far_ref, near_ref, *out_refs):
    for at, ref in enumerate((far_ref, near_ref)):
        total = arrived_ref[at].astype(jnp.float32) + ref[0].astype(jnp.float32)
        out_ref = out_refs[at] if len(out_refs) > 1 else out_refs[0]
        out_ref[at if len(out_refs) == 1 else 0] = total.astype(jnp.bfloat16)


def outer_kernel(info_ref, arrived_ref, terms_ref, *refs):
    term = terms_ref[0].astype(jnp.float32)
    total = term + arrived_ref[0].astype(jnp.float32)
    refs[-1][...] = total.astype(jnp.bfloat16)


def finish_kernel(scale, info_ref, even_ref, odd_ref, terms_ref, *refs):
    out_ref = refs[-1]
    total = even_ref[...].astype(jnp.float32) + odd_ref[0].astype(jnp.float32)
    out_ref[0] = (total + terms_ref[0].astype(jnp.float32)) * scale


def limits(vmem=VMEM_LIMIT, **more):
    return dict(
        compiler_params=pltpu.CompilerParams(vmem_limit_bytes=vmem),
        cost_estimate=pl.CostEstimate(flops=0, bytes_accessed=0, transcendentals=0),
        **more,
    )


SMEM_SPEC = pl.BlockSpec(memory_space=pltpu.SMEM)
HBM_SPEC = pl.BlockSpec(memory_space=pltpu.HBM)
VMEM_SPEC = pl.BlockSpec(memory_space=pltpu.VMEM)


def call(kernel, sizes, ins, outs):
    heads, seg_len, head_dim, count = sizes
    blocks = {
        "c": (seg_len, head_dim),
        "p": (seg_len, 2 * head_dim),
        "r": (1, head_dim),
        "o": (1, 2 * head_dim),
        "R": (count, 2 * head_dim),
        "m": (1, head_dim, head_dim),
        "s": (8, seg_len),
        "n": (16, max(seg_len, head_dim)),
    }

    def shape(kind):
        block = blocks[kind]
        if kind in "msn":
            return (heads * block[0],) + block[1:]
        return (block[0], heads * block[1])

    def of_head(kind, ref, head):
        if kind == "f":
            return ref
        block = blocks[kind]
        if kind in "msn":
            return ref.at[pl.ds(head * block[0], block[0])]
        return ref.at[:, pl.ds(head * block[1], block[1])]

    def all_heads(*refs):
        kinds = list(ins) + [kind for kind, _ in outs]
        for head in range(heads):
            kernel(*[of_head(kind, ref, head) for kind, ref in zip(kinds, refs)])

    return pl.pallas_call(
        all_heads,
        in_specs=[SMEM_SPEC if kind == "f" else VMEM_SPEC for kind in ins],
        out_specs=[VMEM_SPEC] * len(outs),
        out_shape=[jax.ShapeDtypeStruct(shape(kind), dtype) for kind, dtype in outs],
        **limits(),
    )


def local(inputs, w_query, w_key, w_value, gate_bias, cotangent):
    tokens = inputs[0]
    cot = cotangent[0]
    seg_len, model_dim = tokens.shape
    heads = gate_bias.shape[0]
    columns = w_query.shape[1]
    head_dim = columns // heads
    seq_count, seq_at = lax.axis_size("seq"), lax.axis_index("seq")
    dp_count, dp_at = lax.axis_size("dp"), lax.axis_index("dp")
    plane, place = lax.axis_size("head"), lax.axis_index("head")
    part_rows = model_dim // (seq_count * dp_count)
    f32, bf16 = jnp.float32, jnp.bfloat16
    info = jnp.stack([seq_at, 1 - seq_at % 2, dp_at, place]).astype(jnp.int32)

    def shifted(x, by, first=0, last=None):
        last = seq_count - 1 if last is None else last
        pairs = [
            (i, i + by) for i in range(first, last + 1) if 0 <= i + by < seq_count
        ]
        return lax.ppermute(x, "seq", pairs)

    def swapped(x, distance, parity, lowest=0):
        pairs = []
        for i in range(seq_count - distance):
            if (i // distance) % 2 == parity:
                if i >= lowest:
                    pairs.append((i, i + distance))
                if seq_count - 1 - (i + distance) >= lowest:
                    pairs.append((i + distance, i))
        return lax.ppermute(x, "seq", pairs) if pairs else None

    def from_core(x, step):
        return lax.ppermute(x, "dp", [(i, (i + step) % dp_count) for i in range(dp_count)])

    count = -(-(seq_count - 1) // 8) * 8
    sizes = (heads, seg_len, head_dim, count)
    mix = jnp.repeat(jax.nn.sigmoid(gate_bias), head_dim)[None]

    by_swaps = seq_count == 4 and part_rows % 128 == 0
    pieces = 2
    wide_shape = jax.ShapeDtypeStruct((seg_len, 2 * columns), bf16)
    pair, query, even_message, odd_message, row = pl.pallas_call(
        functools.partial(project_kernel, heads),
        in_specs=[SMEM_SPEC] + [HBM_SPEC] * 5,
        out_specs=[VMEM_SPEC] * 5,
        out_shape=[wide_shape] * 4 + [jax.ShapeDtypeStruct((1, 2 * columns), f32)],
        scratch_shapes=[
            pltpu.VMEM((seg_len, model_dim), bf16),
            pltpu.VMEM((3, pieces, model_dim // pieces, columns), bf16),
            pltpu.VMEM((seg_len, columns), bf16),
            pltpu.SemaphoreType.DMA((4 * pieces + 1,)),
        ],
        **limits(48 * 1024 * 1024),
    )(info, tokens, w_key, w_value, w_query, cot)
    even_arrived = swapped(even_message, 1, 0)
    odd_arrived = swapped(odd_message, 1, 1)
    far_rows = [shifted(row, step) for step in range(2, seq_count)]
    odd_arrived, far_rows = lax.optimization_barrier((odd_arrived, far_rows))
    free = jnp.zeros_like(row)
    pad = jnp.zeros((count - seq_count + 1, 2 * columns), f32)
    near = jnp.concatenate([free] + far_rows[:-1] + [free, pad], 0)
    far = jnp.concatenate([free] + far_rows + [pad], 0)

    routes = [
        (distance, parity)
        for distance in range(1, seq_count - 1)
        for parity in range(2)
        if any(
            (i // distance) % 2 == parity and (i > 0 or i + distance < seq_count - 1)
            for i in range(seq_count - distance)
        )
    ]
    routes = [route for route in routes if route != (1, 0)] + [(1, 0)]
    over = "m" * len(routes)
    pair_prev, query_next, memory, grad_memory, row_prev, *sent = call(
        functools.partial(neighbour_kernel, routes),
        sizes,
        "fppRor",
        [("p", bf16)] * 2 + [("m", bf16)] * 2 + [("o", f32)] + [("m", bf16)] * len(routes),
    )(info, even_arrived, odd_arrived, near, row, mix)
    arrived = [swapped(part, *route, lowest=1) for part, route in zip(sent, routes)]
    local_out, grad_att, stats = call(
        attend_kernel, sizes, "fpppr", (("c", f32), ("c", f32), ("s", f32))
    )(info, query, pair, pair_prev, mix)
    if by_swaps:
        all_tokens = [tokens] + [from_core(tokens, step) for step in range(1, dp_count)]
        all_tokens, stats = lax.optimization_barrier((all_tokens, stats))
        token_parts = pl.pallas_call(
            functools.partial(pack_kernel, seq_count, dp_count),
            in_specs=[SMEM_SPEC] + [VMEM_SPEC] * dp_count,
            out_specs=[VMEM_SPEC] * dp_count,
            out_shape=[jax.ShapeDtypeStruct((seq_count * part_rows, seg_len), bf16)] * dp_count,
            **limits(),
        )(info, *all_tokens)
        local_out, token_parts = lax.optimization_barrier((local_out, token_parts))
    blended, grad_query, note = call(
        functools.partial(retrieve_kernel, routes),
        sizes,
        "fpoRrccsm" + over,
        (("c", bf16), ("c", bf16), ("n", f32)),
    )(info, query, row_prev, far, mix, local_out, grad_att, stats, memory, *arrived)
    notes = [shifted(note, -step) for step in range(1, seq_count)]

    def of_cores(grad):
        return [grad] + [from_core(grad, step) for step in range(1, dp_count)]

    def row_blocks(grads):
        return pl.pallas_call(
            row_blocks_kernel,
            in_specs=[SMEM_SPEC] + [VMEM_SPEC] * (2 * dp_count),
            out_specs=[VMEM_SPEC] * 2,
            out_shape=[
                jax.ShapeDtypeStruct((seq_count, part_rows, columns), bf16),
                jax.ShapeDtypeStruct((2, part_rows, columns), bf16),
            ],
            **limits(),
        )(info, *token_parts, *grads)

    grad_scale = 1.0 / math.sqrt(seq_count * dp_count * seg_len)
    block = (part_rows, columns)
    part_shape = jax.ShapeDtypeStruct(block, bf16)
    whole = pl.BlockSpec(block, lambda i, info: (0, 0))
    first = pl.BlockSpec((1,) + block, lambda i, info: (0, 0, 0))

    def on_terms(kernel, ins, outs, out_shape, **more):
        return pl.pallas_call(
            kernel,
            grid_spec=pltpu.PrefetchScalarGridSpec(
                num_scalar_prefetch=1, grid=(1,), in_specs=ins, out_specs=outs
            ),
            out_shape=out_shape,
            **limits(**more),
        )

    def at_block(index):
        return pl.BlockSpec((1,) + block, lambda i, info: (index(info[SEQ]), 0, 0))

    def swapped_ends(first):
        last = seq_count - 1
        return lax.ppermute(first, "seq", [(0, 1), (last, last - 1)])

    def inner_messages(terms, arrived, arrays, *order):
        def inner(info_ref, *refs):
            inner_kernel(*refs[:3], *refs[-arrays:])

        size = (2 // arrays,) + block
        return on_terms(
            inner,
            [
                pl.BlockSpec((2,) + block, lambda i, info: (0, 0, 0)),
                at_block(lambda z: jnp.where(z < 2, 3, 0)),
                at_block(lambda z: jnp.where(z < 2, 2, 1)),
            ]
            + [HBM_SPEC] * len(order),
            [pl.BlockSpec(size, lambda i, info: (0, 0, 0))] * arrays,
            [jax.ShapeDtypeStruct(size, bf16)] * arrays,
        )(info, arrived, terms, terms, *order)

    def end_message(terms, far, *order):
        return on_terms(
            outer_kernel,
            [first, at_block(lambda z: lax.bitwise_xor(z, 1))] + [HBM_SPEC] * len(order),
            whole,
            part_shape,
        )(info, far, terms, *order)

    def finish(terms, even, odd, which, into=()):
        last = odd.shape[0] - 1
        odd_block = pl.BlockSpec((1,) + block, lambda i, info: (last, 0, 0))
        return on_terms(
            functools.partial(finish_kernel, grad_scale),
            [whole, odd_block, at_block(lambda z: z)] + [HBM_SPEC] * len(into),
            pl.BlockSpec((1,) + block, lambda i, info: (which, 0, 0)),
            jax.ShapeDtypeStruct((3,) + block, f32),
            input_output_aliases={4: 0} if into else {},
        )(info, even, odd, terms, *into)

    if by_swaps:
        query_terms, query_first = row_blocks(of_cores(grad_query))
        notes[0], query_terms, query_first = lax.optimization_barrier(
            (notes[0], query_terms, query_first)
        )
        query_ends = swapped_ends(query_first)
    grad_key, grad_value = call(
        functools.partial(key_value_kernel, routes, len(notes)),
        sizes,
        "fppnpr" + "n" * len(notes) + over + "m",
        (("c", bf16), ("c", bf16)),
    )(info, pair, query, note, query_next, mix, *notes, grad_memory, *arrived)
    if not by_swaps:
        contract = (((0,), (0,)), ((), ()))

        def rows_for(core):
            return jnp.concatenate(
                [
                    lax.dynamic_slice_in_dim(
                        tokens, (block * dp_count + core) * part_rows, part_rows, 1
                    )
                    for block in range(seq_count)
                ],
                1,
            )

        token_columns = [rows_for(dp_at)] + [
            from_core(rows_for((dp_at + step) % dp_count), step) for step in range(1, dp_count)
        ]

        def summed(grad):
            grads = [grad] + [from_core(grad, step) for step in range(1, dp_count)]
            terms = sum(
                lax.dot_general(part, term, contract, preferred_element_type=f32)
                for part, term in zip(token_columns, grads)
            ).reshape(seq_count, part_rows, grad.shape[1])

            def block(index):
                index = jnp.clip(index, 0, seq_count - 1)
                return lax.dynamic_index_in_dim(terms, index, 0, False)

            ups = downs = jnp.zeros((part_rows, grad.shape[1]), bf16)
            for turn in range(1, seq_count):
                ahead = seq_count - turn
                ups = shifted((ups + block(seq_at + ahead)).astype(bf16), 1, 0, turn - 1)
                downs = shifted((downs + block(seq_at - ahead)).astype(bf16), -1, ahead)
            return ups + downs + block(seq_at)

        rows = summed(jnp.concatenate([grad_query, grad_key, grad_value], 1)) * grad_scale
        return (blended[None], rows.reshape(part_rows, 3, columns))

    values, keys = lax.optimization_barrier((of_cores(grad_value), of_cores(grad_key)))
    value_terms, value_first = row_blocks(values)
    value_ends = swapped_ends(value_first)
    keys, value_terms = lax.optimization_barrier((keys, value_terms))
    key_terms, key_first = row_blocks(keys)
    key_ends = swapped_ends(key_first)

    (message,) = inner_messages(query_terms, query_ends, 1, key_terms)
    query_odd = swapped(message, 1, 1)
    (message,) = inner_messages(value_terms, value_ends, 1, message)
    value_odd = swapped(message, 1, 1)
    message = end_message(query_terms, query_odd, message)
    query_even = swapped(message, 1, 0)
    messages = inner_messages(key_terms, key_ends, 2, message)
    key_far, key_near = [swapped(message, 1, 1) for message in messages]
    message = end_message(value_terms, value_odd, query_even, *messages)
    value_even = swapped(message, 1, 0)
    message = end_message(key_terms, key_far, message)
    key_even = swapped(message, 1, 0)
    grad_weights = finish(query_terms, query_even, query_odd, 0)
    grad_weights = finish(value_terms, value_even, value_odd, 2, (grad_weights,))
    grad_weights = finish(key_terms, key_even, key_near, 1, (grad_weights,))
    return (blended[None], jnp.transpose(grad_weights, (1, 0, 2)))


def solution(mesh):
    return jax.shard_map(
        local,
        mesh=mesh,
        in_specs=(
            P("dp", "seq", None),
            P(None, "head"),
            P(None, "head"),
            P(None, "head"),
            P("head"),
            P("dp", "seq", "head"),
        ),
        out_specs=(P("dp", "seq", "head"), P(("seq", "dp"), None, "head")),
        check_vma=False,
    )
```

```python
import functools
import math

import jax
import jax.numpy as jnp
from jax import lax
from jax.experimental import pallas as pl
from jax.experimental.pallas import tpu as pltpu
from jax.sharding import PartitionSpec as P

VMEM_LIMIT = 32 * 1024 * 1024
SEQ, EVEN, CORE, PLACE = range(4)


def dot_nn(left, right):
    return lax.dot_general(
        left, right, (((1,), (0,)), ((), ())), preferred_element_type=jnp.float32
    )


def dot_nt(left, right):
    return lax.dot_general(
        left, right, (((1,), (1,)), ((), ())), preferred_element_type=jnp.float32
    )


def dot_tn(left, right):
    return lax.dot_general(
        left, right, (((0,), (0,)), ((), ())), preferred_element_type=jnp.float32
    )


def halves(value):
    high = value.astype(jnp.bfloat16)
    low = (value - high.astype(jnp.float32)).astype(jnp.bfloat16)
    return high, low


def wide(dot, left, right):
    left_high, left_low = halves(left)
    right_high, right_low = halves(right)
    return dot(left_high, right_high) + (dot(left_high, right_low) + dot(left_low, right_high))


def feature(value):
    return jnp.where(value > 0, value + 1.0, jnp.exp(jnp.minimum(value, 0.0)))


def feature_slope(value):
    return jnp.where(value > 0, 1.0, jnp.exp(jnp.minimum(value, 0.0)))


def copies_of(tokens_ref, tokens, weight_refs, weights, sems):
    pieces, depth = weights.shape[1:3]

    def token_copy(piece):
        at = pl.ds(piece * depth, depth)
        return pltpu.make_async_copy(tokens_ref.at[:, at], tokens.at[:, at], sems.at[piece])

    def weight_copy(which, piece):
        return pltpu.make_async_copy(
            weight_refs[which].at[pl.ds(piece * depth, depth)],
            weights.at[which, piece],
            sems.at[(which + 1) * pieces + piece],
        )

    for piece in range(pieces):
        token_copy(piece).start()
        weight_copy(0, piece).start()
    for which in range(1, len(weight_refs)):
        for piece in range(pieces):
            weight_copy(which, piece).start()

    def product(which):
        for piece in range(pieces):
            if which == 0:
                token_copy(piece).wait()
            weight_copy(which, piece).wait()
        parts = []
        half = weights.shape[3] // 2
        for columns in (slice(0, half), slice(half, 2 * half)):
            total = None
            for piece in range(pieces):
                at = slice(piece * depth, (piece + 1) * depth)
                term = dot_nn(tokens[:, at], weights[which, piece, :, columns])
                total = term if total is None else total + term
            parts.append(total.astype(jnp.bfloat16))
        return jnp.concatenate(parts, 1)

    return product


def project_kernel(
    heads,
    info_ref,
    tokens_ref,
    w_key_ref,
    w_value_ref,
    w_query_ref,
    cot_ref,
    pair_ref,
    query_ref,
    even_ref,
    odd_ref,
    row_ref,
    tokens,
    weights,
    cot,
    sems,
):
    product = copies_of(
        tokens_ref, tokens, (w_key_ref, w_value_ref, w_query_ref), weights, sems
    )
    cot_copy = pltpu.make_async_copy(cot_ref, cot, sems.at[sems.shape[0] - 1])
    cot_copy.start()
    head_dim = pair_ref.shape[1] // (2 * heads)
    even = info_ref[EVEN] > 0

    def put(ref, up, at, value):
        ref[:, at] = value

        @pl.when(even == up)
        def _():
            even_ref[:, at] = value

        @pl.when(even != up)
        def _():
            odd_ref[:, at] = value

    for which in range(2):
        result = product(which)
        for head in range(heads):
            part = result[:, head * head_dim : (head + 1) * head_dim]
            at = slice((2 * head + which) * head_dim, (2 * head + which + 1) * head_dim)
            put(pair_ref, True, at, part)
            wide_part = part.astype(jnp.float32)
            if which == 0:
                row_ref[:, at] = jnp.sum(feature(wide_part), axis=0, keepdims=True)
            else:
                row_ref[:, at] = jnp.mean(wide_part, axis=0, keepdims=True)
    query = product(2)
    cot_copy.wait()
    for head in range(heads):
        of_head = slice(head * head_dim, (head + 1) * head_dim)
        at = slice(2 * head * head_dim, (2 * head + 1) * head_dim)
        put(query_ref, False, at, query[:, of_head])
        at = slice((2 * head + 1) * head_dim, (2 * head + 2) * head_dim)
        put(query_ref, False, at, cot[:, of_head])


def lower_end(info_ref, route):
    distance, parity = route
    return lax.rem(lax.div(info_ref[SEQ], distance), 2) == parity


def total_from(info_ref, refs, routes, from_above):
    total = refs[0][0].astype(jnp.float32)
    for ref, route in zip(refs[1:], routes):
        wanted = lower_end(info_ref, route) == from_above
        total = total + jnp.where(wanted, ref[0].astype(jnp.float32), 0.0)
    return total


def neighbour_kernel(routes, info_ref, even_ref, odd_ref, far_ref, row_ref, mix_ref, *refs):
    prev_ref, next_ref, memory_ref, grad_memory_ref, row_prev_ref = refs[:5]
    even = info_ref[EVEN] > 0
    pair = jnp.where(even, odd_ref[...], even_ref[...])
    query = jnp.where(even, even_ref[...], odd_ref[...])
    prev_ref[...] = pair
    next_ref[...] = query
    head_dim = pair.shape[1] // 2
    phi_key = feature(pair[:, :head_dim].astype(jnp.float32))
    value = pair[:, head_dim:].astype(jnp.float32)
    mean = jnp.mean(value, axis=0, keepdims=True)
    centred = (value - mean).astype(jnp.bfloat16)
    memory = dot_tn(phi_key.astype(jnp.bfloat16), centred).astype(jnp.bfloat16)
    norm = jnp.sum(phi_key, axis=0, keepdims=True)
    norm = jnp.where(info_ref[SEQ] > 0, norm, 0.0)
    memory_ref[0] = memory
    row_prev_ref[:, :head_dim] = norm
    row_prev_ref[:, head_dim:] = mean

    phi_query = feature(query[:, :head_dim].astype(jnp.float32))
    norm = norm + jnp.sum(far_ref[:, :head_dim], axis=0, keepdims=True) + row_ref[:, :head_dim]
    denominator = jnp.sum(phi_query * norm, axis=1, keepdims=True) + 1.0
    grad_num = mix_ref[...] * query[:, head_dim:].astype(jnp.float32) / denominator
    grad_memory = dot_tn(phi_query.astype(jnp.bfloat16), grad_num.astype(jnp.bfloat16))
    grad_memory = grad_memory.astype(jnp.bfloat16)
    grad_memory_ref[0] = grad_memory
    for ref, route in zip(refs[5:], routes):
        ref[0] = jnp.where(lower_end(info_ref, route), memory, grad_memory)


def attend_kernel(
    info_ref,
    query_ref,
    pair_ref,
    prev_ref,
    mix_ref,
    out_ref,
    grad_query_ref,
    stats_ref,
):
    seg_len, head_dim = pair_ref.shape[0], pair_ref.shape[1] // 2
    scale = head_dim ** (-0.5)
    query, cot = query_ref[:, :head_dim], query_ref[:, head_dim:]
    key, key_prev = pair_ref[:, :head_dim], prev_ref[:, :head_dim]
    value, value_prev = pair_ref[:, head_dim:], prev_ref[:, head_dim:]
    rows = lax.broadcasted_iota(jnp.int32, (seg_len, seg_len), 0)
    cols = lax.broadcasted_iota(jnp.int32, (seg_len, seg_len), 1)
    score_own = jnp.where(cols <= rows, dot_nt(query, key) * scale, -1e30)
    score_prev = jnp.where(info_ref[SEQ] > 0, dot_nt(query, key_prev) * scale, -1e30)
    row_max = jnp.maximum(
        jnp.max(score_own, axis=1, keepdims=True), jnp.max(score_prev, axis=1, keepdims=True)
    )
    weight_own = jnp.exp(score_own - row_max)
    weight_prev = jnp.exp(score_prev - row_max)
    inverse = 1.0 / (
        jnp.sum(weight_own, axis=1, keepdims=True) + jnp.sum(weight_prev, axis=1, keepdims=True)
    )
    soft_own = weight_own * inverse
    soft_prev = weight_prev * inverse
    out_ref[...] = dot_nn(soft_own.astype(jnp.bfloat16), value) + dot_nn(
        soft_prev.astype(jnp.bfloat16), value_prev
    )
    grad_local = ((1.0 - mix_ref[...]) * cot.astype(jnp.float32)).astype(jnp.bfloat16)
    grad_own = dot_nt(grad_local, value)
    grad_prev = dot_nt(grad_local, value_prev)
    row_dot = jnp.sum(soft_own * grad_own, axis=1, keepdims=True) + jnp.sum(
        soft_prev * grad_prev, axis=1, keepdims=True
    )
    score_grad_own = (soft_own * (grad_own - row_dot) * scale).astype(jnp.bfloat16)
    score_grad_prev = (soft_prev * (grad_prev - row_dot) * scale).astype(jnp.bfloat16)
    grad_query_ref[...] = dot_nn(score_grad_own, key) + dot_nn(score_grad_prev, key_prev)
    lane = lax.broadcasted_iota(jnp.int32, (seg_len, 128), 1)
    stats = jnp.where(
        lane == 0, row_max, jnp.where(lane == 1, inverse, jnp.where(lane == 2, row_dot, 0.0))
    )
    stats_ref[...] = jnp.transpose(stats)[:8]


def retrieve_kernel(
    routes, info_ref, query_ref, row_prev_ref, far_ref, mix_ref, local_ref, grad_att_ref, stats_ref, *refs
):
    blended_ref, grad_query_ref, note_ref = refs[-3:]
    head_dim = query_ref.shape[1] // 2
    query = query_ref[:, :head_dim].astype(jnp.float32)
    phi_query = feature(query)
    free = lax.broadcasted_iota(jnp.int32, far_ref.shape, 0) == 0
    rows = jnp.where(free, row_prev_ref[...], far_ref[...])
    norms = rows[:, :head_dim]
    norm = jnp.sum(norms, axis=0, keepdims=True)
    memory = total_from(info_ref, refs[:-3], routes, False) + wide(dot_tn, norms, rows[:, head_dim:])
    mix = mix_ref[...]
    denominator = jnp.sum(phi_query * norm, axis=1, keepdims=True) + 1.0
    retrieved = wide(dot_nn, phi_query, memory) / denominator
    blended = mix * retrieved + (1.0 - mix) * local_ref[...]
    blended_ref[...] = blended.astype(jnp.bfloat16)
    grad_ret = mix * query_ref[:, head_dim:].astype(jnp.float32)
    grad_num = grad_ret / denominator
    grad_den = -jnp.sum(grad_ret * retrieved, axis=1, keepdims=True) / denominator
    grad_phi = wide(dot_nt, grad_num, memory) + grad_den * norm
    seg_len = query.shape[0]
    note_ref[:8] = stats_ref[...]
    grad_norm = jnp.sum(grad_den * phi_query, axis=0, keepdims=True)
    if seg_len > head_dim:
        filler = jnp.zeros((1, seg_len - head_dim), jnp.float32)
        grad_norm = jnp.concatenate([grad_norm, filler], 1)
    note_ref[8:] = jnp.broadcast_to(grad_norm, (8, grad_norm.shape[1]))
    grad_query = grad_att_ref[...] + grad_phi * feature_slope(query)
    grad_query_ref[...] = grad_query.astype(jnp.bfloat16)


def key_value_kernel(
    routes, notes, info_ref, pair_ref, query_ref, note_ref, query_next_ref, mix_ref, *refs
):
    note_refs, grad_key_ref, grad_value_ref = refs[:notes], refs[-2], refs[-1]
    stats_next = note_refs[0][:8]
    seg_len, head_dim = pair_ref.shape[0], pair_ref.shape[1] // 2
    key, value = pair_ref[:, :head_dim], pair_ref[:, head_dim:]
    scale = head_dim ** (-0.5)
    keep = 1.0 - mix_ref[...]

    def part(query, cot, stats, causal):
        grad_local = (keep * cot.astype(jnp.float32)).astype(jnp.bfloat16)
        score = dot_nt(key, query) * scale
        if causal:
            rows = lax.broadcasted_iota(jnp.int32, score.shape, 0)
            cols = lax.broadcasted_iota(jnp.int32, score.shape, 1)
            score = jnp.where(rows <= cols, score, -1e30)
        soft = jnp.exp(score - stats[0:1]) * stats[1:2]
        grad_value = dot_nn(soft.astype(jnp.bfloat16), grad_local)
        grad_soft = dot_nt(value, grad_local)
        score_grad = (soft * (grad_soft - stats[2:3]) * scale).astype(jnp.bfloat16)
        return dot_nn(score_grad, query), grad_value

    def both(ref, stats, causal):
        return part(ref[:, :head_dim], ref[:, head_dim:], stats, causal)

    own_key, own_value = both(query_ref, note_ref[:8], True)
    next_key, next_value = both(query_next_ref, stats_next, False)
    key_float = key.astype(jnp.float32)
    grad_memory = total_from(info_ref, refs[notes:-2], routes, True).astype(jnp.bfloat16)
    phi_high, phi_low = halves(feature(key_float))
    from_memory = dot_nt(value, grad_memory)
    norm = note_refs[0][8:9, :head_dim]
    for ref in note_refs[1:]:
        norm = norm + ref[8:9, :head_dim]
    from_memory = (from_memory + norm) * feature_slope(key_float)
    grad_key_ref[...] = own_key + next_key + from_memory
    to_value = dot_nn(phi_high, grad_memory) + dot_nn(phi_low, grad_memory)
    grad_value_ref[...] = (own_value + next_value + to_value).astype(jnp.bfloat16)


def join_kernel(heads, pair_ref, rest_ref, *refs):
    note_refs, out_ref = refs[:-1], refs[-1]
    head_dim = pair_ref.shape[1] // (2 * heads)
    for head in range(heads):
        of_head = slice(head * head_dim, (head + 1) * head_dim)
        key = pair_ref[:, 2 * head * head_dim : (2 * head + 1) * head_dim].astype(jnp.float32)
        norm = jnp.zeros((1, head_dim), jnp.float32)
        for ref in note_refs:
            norm = norm + ref[16 * head + 8 : 16 * head + 9, :head_dim]
        grad_key = rest_ref[:, of_head] + norm * feature_slope(key)
        out_ref[:, of_head] = grad_key.astype(jnp.bfloat16)


def pack_kernel(seq_count, dp_count, info_ref, *refs):
    for tokens_ref, out_ref in zip(refs[:dp_count], refs[dp_count:]):
        part_rows = out_ref.shape[0] // seq_count
        own_rows = dp_count * part_rows
        for block in range(seq_count):
            at = pl.multiple_of(info_ref[CORE] * part_rows + block * own_rows, 128)
            out_ref[block * part_rows : (block + 1) * part_rows] = jnp.transpose(
                tokens_ref[:, pl.ds(at, part_rows)]
            )


def row_blocks_kernel(info_ref, *refs):
    *refs, out_ref, first_ref = refs
    count = len(refs) // 2
    blocks, part_rows = out_ref.shape[:2]
    for block in range(blocks):
        rows = slice(block * part_rows, (block + 1) * part_rows)
        total = dot_nn(refs[0][rows], refs[count][...])
        for columns, grad in zip(refs[1:count], refs[count + 1 :]):
            total = total + dot_nn(columns[rows], grad[...])
        total = total.astype(jnp.bfloat16)
        out_ref[block] = total
        place = jnp.where(info_ref[SEQ] == 0, blocks - 1 - block, block)

        @pl.when(place < 2)
        def _(place=place, total=total):
            first_ref[place] = total


def inner_kernel(arrived_ref, far_ref, near_ref, *out_refs):
    for at, ref in enumerate((far_ref, near_ref)):
        total = arrived_ref[at].astype(jnp.float32) + ref[0].astype(jnp.float32)
        out_ref = out_refs[at] if len(out_refs) > 1 else out_refs[0]
        out_ref[at if len(out_refs) == 1 else 0] = total.astype(jnp.bfloat16)


def outer_kernel(info_ref, arrived_ref, terms_ref, *refs):
    term = terms_ref[0].astype(jnp.float32)
    total = term + arrived_ref[0].astype(jnp.float32)
    refs[-1][...] = total.astype(jnp.bfloat16)


def finish_kernel(scale, info_ref, even_ref, odd_ref, terms_ref, *refs):
    out_ref = refs[-1]
    total = even_ref[...].astype(jnp.float32) + odd_ref[0].astype(jnp.float32)
    out_ref[0] = (total + terms_ref[0].astype(jnp.float32)) * scale


def limits(vmem=VMEM_LIMIT, **more):
    return dict(
        compiler_params=pltpu.CompilerParams(vmem_limit_bytes=vmem),
        cost_estimate=pl.CostEstimate(flops=0, bytes_accessed=0, transcendentals=0),
        **more,
    )


SMEM_SPEC = pl.BlockSpec(memory_space=pltpu.SMEM)
HBM_SPEC = pl.BlockSpec(memory_space=pltpu.HBM)
VMEM_SPEC = pl.BlockSpec(memory_space=pltpu.VMEM)


def call(kernel, sizes, ins, outs):
    heads, seg_len, head_dim, count = sizes
    blocks = {
        "c": (seg_len, head_dim),
        "p": (seg_len, 2 * head_dim),
        "r": (1, head_dim),
        "o": (1, 2 * head_dim),
        "R": (count, 2 * head_dim),
        "m": (1, head_dim, head_dim),
        "s": (8, seg_len),
        "n": (16, max(seg_len, head_dim)),
    }

    def shape(kind):
        block = blocks[kind]
        if kind in "msn":
            return (heads * block[0],) + block[1:]
        return (block[0], heads * block[1])

    def of_head(kind, ref, head):
        if kind == "f":
            return ref
        block = blocks[kind]
        if kind in "msn":
            return ref.at[pl.ds(head * block[0], block[0])]
        return ref.at[:, pl.ds(head * block[1], block[1])]

    def all_heads(*refs):
        kinds = list(ins) + [kind for kind, _ in outs]
        for head in range(heads):
            kernel(*[of_head(kind, ref, head) for kind, ref in zip(kinds, refs)])

    return pl.pallas_call(
        all_heads,
        in_specs=[SMEM_SPEC if kind == "f" else VMEM_SPEC for kind in ins],
        out_specs=[VMEM_SPEC] * len(outs),
        out_shape=[jax.ShapeDtypeStruct(shape(kind), dtype) for kind, dtype in outs],
        **limits(),
    )


def local(inputs, w_query, w_key, w_value, gate_bias, cotangent):
    tokens = inputs[0]
    cot = cotangent[0]
    seg_len, model_dim = tokens.shape
    heads = gate_bias.shape[0]
    columns = w_query.shape[1]
    head_dim = columns // heads
    seq_count, seq_at = lax.axis_size("seq"), lax.axis_index("seq")
    dp_count, dp_at = lax.axis_size("dp"), lax.axis_index("dp")
    plane, place = lax.axis_size("head"), lax.axis_index("head")
    part_rows = model_dim // (seq_count * dp_count)
    f32, bf16 = jnp.float32, jnp.bfloat16
    info = jnp.stack([seq_at, 1 - seq_at % 2, dp_at, place]).astype(jnp.int32)

    def shifted(x, by, first=0, last=None):
        last = seq_count - 1 if last is None else last
        pairs = [
            (i, i + by) for i in range(first, last + 1) if 0 <= i + by < seq_count
        ]
        return lax.ppermute(x, "seq", pairs)

    def swapped(x, distance, parity, lowest=0):
        pairs = []
        for i in range(seq_count - distance):
            if (i // distance) % 2 == parity:
                if i >= lowest:
                    pairs.append((i, i + distance))
                if seq_count - 1 - (i + distance) >= lowest:
                    pairs.append((i + distance, i))
        return lax.ppermute(x, "seq", pairs) if pairs else None

    def from_core(x, step):
        return lax.ppermute(x, "dp", [(i, (i + step) % dp_count) for i in range(dp_count)])

    count = -(-(seq_count - 1) // 8) * 8
    sizes = (heads, seg_len, head_dim, count)
    mix = jnp.repeat(jax.nn.sigmoid(gate_bias), head_dim)[None]

    by_swaps = seq_count == 4 and part_rows % 128 == 0
    pieces = 2
    wide_shape = jax.ShapeDtypeStruct((seg_len, 2 * columns), bf16)
    pair, query, even_message, odd_message, row = pl.pallas_call(
        functools.partial(project_kernel, heads),
        in_specs=[SMEM_SPEC] + [HBM_SPEC] * 5,
        out_specs=[VMEM_SPEC] * 5,
        out_shape=[wide_shape] * 4 + [jax.ShapeDtypeStruct((1, 2 * columns), f32)],
        scratch_shapes=[
            pltpu.VMEM((seg_len, model_dim), bf16),
            pltpu.VMEM((3, pieces, model_dim // pieces, columns), bf16),
            pltpu.VMEM((seg_len, columns), bf16),
            pltpu.SemaphoreType.DMA((4 * pieces + 1,)),
        ],
        **limits(48 * 1024 * 1024),
    )(info, tokens, w_key, w_value, w_query, cot)
    even_arrived = swapped(even_message, 1, 0)
    odd_arrived = swapped(odd_message, 1, 1)
    far_rows = [shifted(row, step) for step in range(2, seq_count)]
    odd_arrived, far_rows = lax.optimization_barrier((odd_arrived, far_rows))
    free = jnp.zeros_like(row)
    pad = jnp.zeros((count - seq_count + 1, 2 * columns), f32)
    near = jnp.concatenate([free] + far_rows[:-1] + [free, pad], 0)
    far = jnp.concatenate([free] + far_rows + [pad], 0)

    routes = [
        (distance, parity)
        for distance in range(1, seq_count - 1)
        for parity in range(2)
        if any(
            (i // distance) % 2 == parity and (i > 0 or i + distance < seq_count - 1)
            for i in range(seq_count - distance)
        )
    ]
    routes = [route for route in routes if route != (1, 0)] + [(1, 0)]
    over = "m" * len(routes)
    pair_prev, query_next, memory, grad_memory, row_prev, *sent = call(
        functools.partial(neighbour_kernel, routes),
        sizes,
        "fppRor",
        [("p", bf16)] * 2 + [("m", bf16)] * 2 + [("o", f32)] + [("m", bf16)] * len(routes),
    )(info, even_arrived, odd_arrived, near, row, mix)
    arrived = [swapped(part, *route, lowest=1) for part, route in zip(sent, routes)]
    local_out, grad_att, stats = call(
        attend_kernel, sizes, "fpppr", (("c", f32), ("c", f32), ("s", f32))
    )(info, query, pair, pair_prev, mix)
    if by_swaps:
        all_tokens = [tokens] + [from_core(tokens, step) for step in range(1, dp_count)]
        all_tokens, stats = lax.optimization_barrier((all_tokens, stats))
        token_parts = pl.pallas_call(
            functools.partial(pack_kernel, seq_count, dp_count),
            in_specs=[SMEM_SPEC] + [VMEM_SPEC] * dp_count,
            out_specs=[VMEM_SPEC] * dp_count,
            out_shape=[jax.ShapeDtypeStruct((seq_count * part_rows, seg_len), bf16)] * dp_count,
            **limits(),
        )(info, *all_tokens)
        local_out, token_parts = lax.optimization_barrier((local_out, token_parts))
    blended, grad_query, note = call(
        functools.partial(retrieve_kernel, routes),
        sizes,
        "fpoRrccsm" + over,
        (("c", bf16), ("c", bf16), ("n", f32)),
    )(info, query, row_prev, far, mix, local_out, grad_att, stats, memory, *arrived)
    notes = [shifted(note, -step) for step in range(1, seq_count)]

    def of_cores(grad):
        return [grad] + [from_core(grad, step) for step in range(1, dp_count)]

    def row_blocks(grads):
        return pl.pallas_call(
            row_blocks_kernel,
            in_specs=[SMEM_SPEC] + [VMEM_SPEC] * (2 * dp_count),
            out_specs=[VMEM_SPEC] * 2,
            out_shape=[
                jax.ShapeDtypeStruct((seq_count, part_rows, columns), bf16),
                jax.ShapeDtypeStruct((2, part_rows, columns), bf16),
            ],
            **limits(),
        )(info, *token_parts, *grads)

    grad_scale = 1.0 / math.sqrt(seq_count * dp_count * seg_len)
    block = (part_rows, columns)
    part_shape = jax.ShapeDtypeStruct(block, bf16)
    whole = pl.BlockSpec(block, lambda i, info: (0, 0))
    first = pl.BlockSpec((1,) + block, lambda i, info: (0, 0, 0))

    def on_terms(kernel, ins, outs, out_shape, **more):
        return pl.pallas_call(
            kernel,
            grid_spec=pltpu.PrefetchScalarGridSpec(
                num_scalar_prefetch=1, grid=(1,), in_specs=ins, out_specs=outs
            ),
            out_shape=out_shape,
            **limits(**more),
        )

    def at_block(index):
        return pl.BlockSpec((1,) + block, lambda i, info: (index(info[SEQ]), 0, 0))

    def swapped_ends(first):
        last = seq_count - 1
        return lax.ppermute(first, "seq", [(0, 1), (last, last - 1)])

    def inner_messages(terms, arrived, arrays, *order):
        def inner(info_ref, *refs):
            inner_kernel(*refs[:3], *refs[-arrays:])

        size = (2 // arrays,) + block
        return on_terms(
            inner,
            [
                pl.BlockSpec((2,) + block, lambda i, info: (0, 0, 0)),
                at_block(lambda z: jnp.where(z < 2, 3, 0)),
                at_block(lambda z: jnp.where(z < 2, 2, 1)),
            ]
            + [HBM_SPEC] * len(order),
            [pl.BlockSpec(size, lambda i, info: (0, 0, 0))] * arrays,
            [jax.ShapeDtypeStruct(size, bf16)] * arrays,
        )(info, arrived, terms, terms, *order)

    def end_message(terms, far, *order):
        return on_terms(
            outer_kernel,
            [first, at_block(lambda z: lax.bitwise_xor(z, 1))] + [HBM_SPEC] * len(order),
            whole,
            part_shape,
        )(info, far, terms, *order)

    def finish(terms, even, odd, which, into=()):
        last = odd.shape[0] - 1
        odd_block = pl.BlockSpec((1,) + block, lambda i, info: (last, 0, 0))
        return on_terms(
            functools.partial(finish_kernel, grad_scale),
            [whole, odd_block, at_block(lambda z: z)] + [HBM_SPEC] * len(into),
            pl.BlockSpec((1,) + block, lambda i, info: (which, 0, 0)),
            jax.ShapeDtypeStruct((3,) + block, f32),
            input_output_aliases={4: 0} if into else {},
        )(info, even, odd, terms, *into)

    if by_swaps:
        query_terms, query_first = row_blocks(of_cores(grad_query))
        notes[0], query_terms, query_first = lax.optimization_barrier(
            (notes[0], query_terms, query_first)
        )
        notes[1:], query_first = lax.optimization_barrier((notes[1:], query_first))
        query_ends = swapped_ends(query_first)
    key_rest, grad_value = call(
        functools.partial(key_value_kernel, routes, 1),
        sizes,
        "fppnprn" + over + "m",
        (("c", f32), ("c", bf16)),
    )(info, pair, query, note, query_next, mix, notes[0], grad_memory, *arrived)
    grad_key = pl.pallas_call(
        functools.partial(join_kernel, heads),
        out_shape=jax.ShapeDtypeStruct((seg_len, columns), bf16),
        **limits(),
    )(pair, key_rest, *notes[1:])
    if not by_swaps:
        contract = (((0,), (0,)), ((), ()))

        def rows_for(core):
            return jnp.concatenate(
                [
                    lax.dynamic_slice_in_dim(
                        tokens, (block * dp_count + core) * part_rows, part_rows, 1
                    )
                    for block in range(seq_count)
                ],
                1,
            )

        token_columns = [rows_for(dp_at)] + [
            from_core(rows_for((dp_at + step) % dp_count), step) for step in range(1, dp_count)
        ]

        def summed(grad):
            grads = [grad] + [from_core(grad, step) for step in range(1, dp_count)]
            terms = sum(
                lax.dot_general(part, term, contract, preferred_element_type=f32)
                for part, term in zip(token_columns, grads)
            ).reshape(seq_count, part_rows, grad.shape[1])

            def block(index):
                index = jnp.clip(index, 0, seq_count - 1)
                return lax.dynamic_index_in_dim(terms, index, 0, False)

            ups = downs = jnp.zeros((part_rows, grad.shape[1]), bf16)
            for turn in range(1, seq_count):
                ahead = seq_count - turn
                ups = shifted((ups + block(seq_at + ahead)).astype(bf16), 1, 0, turn - 1)
                downs = shifted((downs + block(seq_at - ahead)).astype(bf16), -1, ahead)
            return ups + downs + block(seq_at)

        rows = summed(jnp.concatenate([grad_query, grad_key, grad_value], 1)) * grad_scale
        return (blended[None], rows.reshape(part_rows, 3, columns))

    values, grad_key = lax.optimization_barrier((of_cores(grad_value), grad_key))
    keys = of_cores(grad_key)
    value_terms, value_first = row_blocks(values)
    value_ends = swapped_ends(value_first)
    keys, value_terms = lax.optimization_barrier((keys, value_terms))
    key_terms, key_first = row_blocks(keys)
    key_ends = swapped_ends(key_first)

    (message,) = inner_messages(query_terms, query_ends, 1, key_terms)
    query_odd = swapped(message, 1, 1)
    (message,) = inner_messages(value_terms, value_ends, 1, message)
    value_odd = swapped(message, 1, 1)
    message = end_message(query_terms, query_odd, message)
    query_even = swapped(message, 1, 0)
    messages = inner_messages(key_terms, key_ends, 2, message)
    key_far, key_near = [swapped(message, 1, 1) for message in messages]
    message = end_message(value_terms, value_odd, query_even, *messages)
    value_even = swapped(message, 1, 0)
    message = end_message(key_terms, key_far, message)
    key_even = swapped(message, 1, 0)
    grad_weights = finish(query_terms, query_even, query_odd, 0)
    grad_weights = finish(value_terms, value_even, value_odd, 2, (grad_weights,))
    grad_weights = finish(key_terms, key_even, key_near, 1, (grad_weights,))
    return (blended[None], jnp.transpose(grad_weights, (1, 0, 2)))


def solution(mesh):
    return jax.shard_map(
        local,
        mesh=mesh,
        in_specs=(
            P("dp", "seq", None),
            P(None, "head"),
            P(None, "head"),
            P(None, "head"),
            P("head"),
            P("dp", "seq", "head"),
        ),
        out_specs=(P("dp", "seq", "head"), P(("seq", "dp"), None, "head")),
        check_vma=False,
    )
```

```python
import functools
import math

import jax
import jax.numpy as jnp
from jax import lax
from jax.experimental import pallas as pl
from jax.experimental.pallas import tpu as pltpu
from jax.sharding import PartitionSpec as P

VMEM_LIMIT = 32 * 1024 * 1024
SEQ, EVEN, CORE, PLACE = range(4)


def dot_nn(left, right):
    return lax.dot_general(
        left, right, (((1,), (0,)), ((), ())), preferred_element_type=jnp.float32
    )


def dot_nt(left, right):
    return lax.dot_general(
        left, right, (((1,), (1,)), ((), ())), preferred_element_type=jnp.float32
    )


def dot_tn(left, right):
    return lax.dot_general(
        left, right, (((0,), (0,)), ((), ())), preferred_element_type=jnp.float32
    )


def halves(value):
    high = value.astype(jnp.bfloat16)
    low = (value - high.astype(jnp.float32)).astype(jnp.bfloat16)
    return high, low


def wide(dot, left, right):
    left_high, left_low = halves(left)
    right_high, right_low = halves(right)
    return dot(left_high, right_high) + (dot(left_high, right_low) + dot(left_low, right_high))


def feature(value):
    return jnp.where(value > 0, value + 1.0, jnp.exp(jnp.minimum(value, 0.0)))


def feature_slope(value):
    return jnp.where(value > 0, 1.0, jnp.exp(jnp.minimum(value, 0.0)))


def copies_of(tokens_ref, tokens, weight_refs, weights, sems):
    pieces, depth = weights.shape[1:3]

    def token_copy(piece):
        at = pl.ds(piece * depth, depth)
        return pltpu.make_async_copy(tokens_ref.at[:, at], tokens.at[:, at], sems.at[piece])

    def weight_copy(which, piece):
        return pltpu.make_async_copy(
            weight_refs[which].at[pl.ds(piece * depth, depth)],
            weights.at[which, piece],
            sems.at[(which + 1) * pieces + piece],
        )

    for piece in range(pieces):
        token_copy(piece).start()
        weight_copy(0, piece).start()
    for which in range(1, len(weight_refs)):
        for piece in range(pieces):
            weight_copy(which, piece).start()

    def product(which):
        for piece in range(pieces):
            if which == 0:
                token_copy(piece).wait()
            weight_copy(which, piece).wait()
        parts = []
        half = weights.shape[3] // 2
        for columns in (slice(0, half), slice(half, 2 * half)):
            total = None
            for piece in range(pieces):
                at = slice(piece * depth, (piece + 1) * depth)
                term = dot_nn(tokens[:, at], weights[which, piece, :, columns])
                total = term if total is None else total + term
            parts.append(total.astype(jnp.bfloat16))
        return jnp.concatenate(parts, 1)

    return product


def project_kernel(
    heads,
    info_ref,
    tokens_ref,
    w_key_ref,
    w_value_ref,
    w_query_ref,
    cot_ref,
    pair_ref,
    query_ref,
    even_ref,
    odd_ref,
    row_ref,
    tokens,
    weights,
    cot,
    sems,
):
    product = copies_of(
        tokens_ref, tokens, (w_key_ref, w_value_ref, w_query_ref), weights, sems
    )
    cot_copy = pltpu.make_async_copy(cot_ref, cot, sems.at[sems.shape[0] - 1])
    cot_copy.start()
    head_dim = pair_ref.shape[1] // (2 * heads)
    even = info_ref[EVEN] > 0

    def put(ref, up, at, value):
        ref[:, at] = value

        @pl.when(even == up)
        def _():
            even_ref[:, at] = value

        @pl.when(even != up)
        def _():
            odd_ref[:, at] = value

    for which in range(2):
        result = product(which)
        for head in range(heads):
            part = result[:, head * head_dim : (head + 1) * head_dim]
            at = slice((2 * head + which) * head_dim, (2 * head + which + 1) * head_dim)
            put(pair_ref, True, at, part)
            wide_part = part.astype(jnp.float32)
            if which == 0:
                row_ref[:, at] = jnp.sum(feature(wide_part), axis=0, keepdims=True)
            else:
                row_ref[:, at] = jnp.mean(wide_part, axis=0, keepdims=True)
    query = product(2)
    cot_copy.wait()
    for head in range(heads):
        of_head = slice(head * head_dim, (head + 1) * head_dim)
        at = slice(2 * head * head_dim, (2 * head + 1) * head_dim)
        put(query_ref, False, at, query[:, of_head])
        at = slice((2 * head + 1) * head_dim, (2 * head + 2) * head_dim)
        put(query_ref, False, at, cot[:, of_head])


def lower_end(info_ref, route):
    distance, parity = route
    return lax.rem(lax.div(info_ref[SEQ], distance), 2) == parity


def total_from(info_ref, refs, routes, from_above):
    total = refs[0][0].astype(jnp.float32)
    for ref, route in zip(refs[1:], routes):
        wanted = lower_end(info_ref, route) == from_above
        total = total + jnp.where(wanted, ref[0].astype(jnp.float32), 0.0)
    return total


def neighbour_kernel(routes, info_ref, even_ref, odd_ref, far_ref, row_ref, mix_ref, *refs):
    prev_ref, next_ref, memory_ref, grad_memory_ref, row_prev_ref = refs[:5]
    even = info_ref[EVEN] > 0
    pair = jnp.where(even, odd_ref[...], even_ref[...])
    query = jnp.where(even, even_ref[...], odd_ref[...])
    prev_ref[...] = pair
    next_ref[...] = query
    head_dim = pair.shape[1] // 2
    phi_key = feature(pair[:, :head_dim].astype(jnp.float32))
    value = pair[:, head_dim:].astype(jnp.float32)
    mean = jnp.mean(value, axis=0, keepdims=True)
    centred = (value - mean).astype(jnp.bfloat16)
    memory = dot_tn(phi_key.astype(jnp.bfloat16), centred).astype(jnp.bfloat16)
    norm = jnp.sum(phi_key, axis=0, keepdims=True)
    norm = jnp.where(info_ref[SEQ] > 0, norm, 0.0)
    memory_ref[0] = memory
    row_prev_ref[:, :head_dim] = norm
    row_prev_ref[:, head_dim:] = mean

    phi_query = feature(query[:, :head_dim].astype(jnp.float32))
    norm = norm + jnp.sum(far_ref[:, :head_dim], axis=0, keepdims=True) + row_ref[:, :head_dim]
    denominator = jnp.sum(phi_query * norm, axis=1, keepdims=True) + 1.0
    grad_num = mix_ref[...] * query[:, head_dim:].astype(jnp.float32) / denominator
    grad_memory = dot_tn(phi_query.astype(jnp.bfloat16), grad_num.astype(jnp.bfloat16))
    grad_memory = grad_memory.astype(jnp.bfloat16)
    grad_memory_ref[0] = grad_memory
    for ref, route in zip(refs[5:], routes):
        ref[0] = jnp.where(lower_end(info_ref, route), memory, grad_memory)


def attend_kernel(
    info_ref,
    query_ref,
    pair_ref,
    prev_ref,
    mix_ref,
    out_ref,
    grad_query_ref,
    stats_ref,
):
    seg_len, head_dim = pair_ref.shape[0], pair_ref.shape[1] // 2
    scale = head_dim ** (-0.5)
    query, cot = query_ref[:, :head_dim], query_ref[:, head_dim:]
    key, key_prev = pair_ref[:, :head_dim], prev_ref[:, :head_dim]
    value, value_prev = pair_ref[:, head_dim:], prev_ref[:, head_dim:]
    rows = lax.broadcasted_iota(jnp.int32, (seg_len, seg_len), 0)
    cols = lax.broadcasted_iota(jnp.int32, (seg_len, seg_len), 1)
    score_own = jnp.where(cols <= rows, dot_nt(query, key) * scale, -1e30)
    score_prev = jnp.where(info_ref[SEQ] > 0, dot_nt(query, key_prev) * scale, -1e30)
    row_max = jnp.maximum(
        jnp.max(score_own, axis=1, keepdims=True), jnp.max(score_prev, axis=1, keepdims=True)
    )
    weight_own = jnp.exp(score_own - row_max)
    weight_prev = jnp.exp(score_prev - row_max)
    inverse = 1.0 / (
        jnp.sum(weight_own, axis=1, keepdims=True) + jnp.sum(weight_prev, axis=1, keepdims=True)
    )
    soft_own = weight_own * inverse
    soft_prev = weight_prev * inverse
    out_ref[...] = dot_nn(soft_own.astype(jnp.bfloat16), value) + dot_nn(
        soft_prev.astype(jnp.bfloat16), value_prev
    )
    grad_local = ((1.0 - mix_ref[...]) * cot.astype(jnp.float32)).astype(jnp.bfloat16)
    grad_own = dot_nt(grad_local, value)
    grad_prev = dot_nt(grad_local, value_prev)
    row_dot = jnp.sum(soft_own * grad_own, axis=1, keepdims=True) + jnp.sum(
        soft_prev * grad_prev, axis=1, keepdims=True
    )
    score_grad_own = (soft_own * (grad_own - row_dot) * scale).astype(jnp.bfloat16)
    score_grad_prev = (soft_prev * (grad_prev - row_dot) * scale).astype(jnp.bfloat16)
    grad_query_ref[...] = dot_nn(score_grad_own, key) + dot_nn(score_grad_prev, key_prev)
    lane = lax.broadcasted_iota(jnp.int32, (seg_len, 128), 1)
    stats = jnp.where(
        lane == 0, row_max, jnp.where(lane == 1, inverse, jnp.where(lane == 2, row_dot, 0.0))
    )
    stats_ref[...] = jnp.transpose(stats)[:8]


def retrieve_kernel(
    routes, info_ref, query_ref, row_prev_ref, far_ref, mix_ref, local_ref, grad_att_ref, stats_ref, *refs
):
    blended_ref, grad_query_ref, note_ref = refs[-3:]
    head_dim = query_ref.shape[1] // 2
    query = query_ref[:, :head_dim].astype(jnp.float32)
    phi_query = feature(query)
    free = lax.broadcasted_iota(jnp.int32, far_ref.shape, 0) == 0
    rows = jnp.where(free, row_prev_ref[...], far_ref[...])
    norms = rows[:, :head_dim]
    norm = jnp.sum(norms, axis=0, keepdims=True)
    memory = total_from(info_ref, refs[:-3], routes, False) + wide(dot_tn, norms, rows[:, head_dim:])
    mix = mix_ref[...]
    denominator = jnp.sum(phi_query * norm, axis=1, keepdims=True) + 1.0
    retrieved = wide(dot_nn, phi_query, memory) / denominator
    blended = mix * retrieved + (1.0 - mix) * local_ref[...]
    blended_ref[...] = blended.astype(jnp.bfloat16)
    grad_ret = mix * query_ref[:, head_dim:].astype(jnp.float32)
    grad_num = grad_ret / denominator
    grad_den = -jnp.sum(grad_ret * retrieved, axis=1, keepdims=True) / denominator
    grad_phi = wide(dot_nt, grad_num, memory) + grad_den * norm
    seg_len = query.shape[0]
    note_ref[:8] = stats_ref[...]
    grad_norm = jnp.sum(grad_den * phi_query, axis=0, keepdims=True)
    if seg_len > head_dim:
        filler = jnp.zeros((1, seg_len - head_dim), jnp.float32)
        grad_norm = jnp.concatenate([grad_norm, filler], 1)
    note_ref[8:] = jnp.broadcast_to(grad_norm, (8, grad_norm.shape[1]))
    grad_query = grad_att_ref[...] + grad_phi * feature_slope(query)
    grad_query_ref[...] = grad_query.astype(jnp.bfloat16)


def key_value_kernel(
    routes, notes, info_ref, pair_ref, query_ref, note_ref, query_next_ref, mix_ref, *refs
):
    note_refs, grad_key_ref, grad_value_ref = refs[:notes], refs[-2], refs[-1]
    stats_next = note_refs[0][:8]
    seg_len, head_dim = pair_ref.shape[0], pair_ref.shape[1] // 2
    key, value = pair_ref[:, :head_dim], pair_ref[:, head_dim:]
    scale = head_dim ** (-0.5)
    keep = 1.0 - mix_ref[...]

    def part(query, cot, stats, causal):
        grad_local = (keep * cot.astype(jnp.float32)).astype(jnp.bfloat16)
        score = dot_nt(key, query) * scale
        if causal:
            rows = lax.broadcasted_iota(jnp.int32, score.shape, 0)
            cols = lax.broadcasted_iota(jnp.int32, score.shape, 1)
            score = jnp.where(rows <= cols, score, -1e30)
        soft = jnp.exp(jnp.minimum(score - stats[0:1], 0.0)) * stats[1:2]
        grad_value = dot_nn(soft.astype(jnp.bfloat16), grad_local)
        grad_soft = dot_nt(value, grad_local)
        score_grad = (soft * (grad_soft - stats[2:3]) * scale).astype(jnp.bfloat16)
        return dot_nn(score_grad, query), grad_value

    def both(ref, stats, causal):
        return part(ref[:, :head_dim], ref[:, head_dim:], stats, causal)

    own_key, own_value = both(query_ref, note_ref[:8], True)
    next_key, next_value = both(query_next_ref, stats_next, False)
    key_float = key.astype(jnp.float32)
    grad_memory = total_from(info_ref, refs[notes:-2], routes, True).astype(jnp.bfloat16)
    phi_high, phi_low = halves(feature(key_float))
    from_memory = dot_nt(value, grad_memory)
    norm = note_refs[0][8:9, :head_dim]
    for ref in note_refs[1:]:
        norm = norm + ref[8:9, :head_dim]
    from_memory = (from_memory + norm) * feature_slope(key_float)
    grad_key_ref[...] = own_key + next_key + from_memory
    to_value = dot_nn(phi_high, grad_memory) + dot_nn(phi_low, grad_memory)
    grad_value_ref[...] = (own_value + next_value + to_value).astype(jnp.bfloat16)


def join_kernel(heads, pair_ref, rest_ref, *refs):
    note_refs, out_ref = refs[:-1], refs[-1]
    head_dim = pair_ref.shape[1] // (2 * heads)
    for head in range(heads):
        of_head = slice(head * head_dim, (head + 1) * head_dim)
        key = pair_ref[:, 2 * head * head_dim : (2 * head + 1) * head_dim].astype(jnp.float32)
        norm = jnp.zeros((1, head_dim), jnp.float32)
        for ref in note_refs:
            norm = norm + ref[16 * head + 8 : 16 * head + 9, :head_dim]
        grad_key = rest_ref[:, of_head] + norm * feature_slope(key)
        out_ref[:, of_head] = grad_key.astype(jnp.bfloat16)


def pack_kernel(seq_count, dp_count, info_ref, *refs):
    for tokens_ref, out_ref in zip(refs[:dp_count], refs[dp_count:]):
        part_rows = out_ref.shape[0] // seq_count
        own_rows = dp_count * part_rows
        for block in range(seq_count):
            at = pl.multiple_of(info_ref[CORE] * part_rows + block * own_rows, 128)
            out_ref[block * part_rows : (block + 1) * part_rows] = jnp.transpose(
                tokens_ref[:, pl.ds(at, part_rows)]
            )


def row_blocks_kernel(info_ref, *refs):
    *refs, out_ref, first_ref = refs
    count = len(refs) // 2
    blocks, part_rows = out_ref.shape[:2]
    for block in range(blocks):
        rows = slice(block * part_rows, (block + 1) * part_rows)
        total = dot_nn(refs[0][rows], refs[count][...])
        for columns, grad in zip(refs[1:count], refs[count + 1 :]):
            total = total + dot_nn(columns[rows], grad[...])
        total = total.astype(jnp.bfloat16)
        out_ref[block] = total
        place = jnp.where(info_ref[SEQ] == 0, blocks - 1 - block, block)

        @pl.when(place < 2)
        def _(place=place, total=total):
            first_ref[place] = total


def inner_kernel(arrived_ref, far_ref, near_ref, *out_refs):
    for at, ref in enumerate((far_ref, near_ref)):
        total = arrived_ref[at].astype(jnp.float32) + ref[0].astype(jnp.float32)
        out_ref = out_refs[at] if len(out_refs) > 1 else out_refs[0]
        out_ref[at if len(out_refs) == 1 else 0] = total.astype(jnp.bfloat16)


def outer_kernel(info_ref, arrived_ref, terms_ref, *refs):
    term = terms_ref[0].astype(jnp.float32)
    total = term + arrived_ref[0].astype(jnp.float32)
    refs[-1][...] = total.astype(jnp.bfloat16)


def finish_kernel(scale, info_ref, even_ref, odd_ref, terms_ref, *refs):
    out_ref = refs[-1]
    total = even_ref[...].astype(jnp.float32) + odd_ref[0].astype(jnp.float32)
    out_ref[0] = (total + terms_ref[0].astype(jnp.float32)) * scale


def limits(vmem=VMEM_LIMIT, **more):
    return dict(
        compiler_params=pltpu.CompilerParams(vmem_limit_bytes=vmem),
        cost_estimate=pl.CostEstimate(flops=0, bytes_accessed=0, transcendentals=0),
        **more,
    )


SMEM_SPEC = pl.BlockSpec(memory_space=pltpu.SMEM)
HBM_SPEC = pl.BlockSpec(memory_space=pltpu.HBM)
VMEM_SPEC = pl.BlockSpec(memory_space=pltpu.VMEM)


def call(kernel, sizes, ins, outs):
    heads, seg_len, head_dim, count = sizes
    blocks = {
        "c": (seg_len, head_dim),
        "p": (seg_len, 2 * head_dim),
        "r": (1, head_dim),
        "o": (1, 2 * head_dim),
        "R": (count, 2 * head_dim),
        "m": (1, head_dim, head_dim),
        "s": (8, seg_len),
        "n": (16, max(seg_len, head_dim)),
    }

    def shape(kind):
        block = blocks[kind]
        if kind in "msn":
            return (heads * block[0],) + block[1:]
        return (block[0], heads * block[1])

    def of_head(kind, ref, head):
        if kind == "f":
            return ref
        block = blocks[kind]
        if kind in "msn":
            return ref.at[pl.ds(head * block[0], block[0])]
        return ref.at[:, pl.ds(head * block[1], block[1])]

    def all_heads(*refs):
        kinds = list(ins) + [kind for kind, _ in outs]
        for head in range(heads):
            kernel(*[of_head(kind, ref, head) for kind, ref in zip(kinds, refs)])

    return pl.pallas_call(
        all_heads,
        in_specs=[SMEM_SPEC if kind == "f" else VMEM_SPEC for kind in ins],
        out_specs=[VMEM_SPEC] * len(outs),
        out_shape=[jax.ShapeDtypeStruct(shape(kind), dtype) for kind, dtype in outs],
        **limits(),
    )


def local(inputs, w_query, w_key, w_value, gate_bias, cotangent):
    tokens = inputs[0]
    cot = cotangent[0]
    seg_len, model_dim = tokens.shape
    heads = gate_bias.shape[0]
    columns = w_query.shape[1]
    head_dim = columns // heads
    seq_count, seq_at = lax.axis_size("seq"), lax.axis_index("seq")
    dp_count, dp_at = lax.axis_size("dp"), lax.axis_index("dp")
    plane, place = lax.axis_size("head"), lax.axis_index("head")
    part_rows = model_dim // (seq_count * dp_count)
    f32, bf16 = jnp.float32, jnp.bfloat16
    info = jnp.stack([seq_at, 1 - seq_at % 2, dp_at, place]).astype(jnp.int32)

    def shifted(x, by, first=0, last=None):
        last = seq_count - 1 if last is None else last
        pairs = [
            (i, i + by) for i in range(first, last + 1) if 0 <= i + by < seq_count
        ]
        return lax.ppermute(x, "seq", pairs)

    def swapped(x, distance, parity, lowest=0):
        pairs = []
        for i in range(seq_count - distance):
            if (i // distance) % 2 == parity:
                if i >= lowest:
                    pairs.append((i, i + distance))
                if seq_count - 1 - (i + distance) >= lowest:
                    pairs.append((i + distance, i))
        return lax.ppermute(x, "seq", pairs) if pairs else None

    def from_core(x, step):
        return lax.ppermute(x, "dp", [(i, (i + step) % dp_count) for i in range(dp_count)])

    count = -(-(seq_count - 1) // 8) * 8
    sizes = (heads, seg_len, head_dim, count)
    mix = jnp.repeat(jax.nn.sigmoid(gate_bias), head_dim)[None]

    by_swaps = seq_count == 4 and part_rows % 128 == 0
    pieces = 2
    wide_shape = jax.ShapeDtypeStruct((seg_len, 2 * columns), bf16)
    pair, query, even_message, odd_message, row = pl.pallas_call(
        functools.partial(project_kernel, heads),
        in_specs=[SMEM_SPEC] + [HBM_SPEC] * 5,
        out_specs=[VMEM_SPEC] * 5,
        out_shape=[wide_shape] * 4 + [jax.ShapeDtypeStruct((1, 2 * columns), f32)],
        scratch_shapes=[
            pltpu.VMEM((seg_len, model_dim), bf16),
            pltpu.VMEM((3, pieces, model_dim // pieces, columns), bf16),
            pltpu.VMEM((seg_len, columns), bf16),
            pltpu.SemaphoreType.DMA((4 * pieces + 1,)),
        ],
        **limits(48 * 1024 * 1024),
    )(info, tokens, w_key, w_value, w_query, cot)
    even_arrived = swapped(even_message, 1, 0)
    odd_arrived = swapped(odd_message, 1, 1)
    far_rows = [shifted(row, step) for step in range(2, seq_count)]
    odd_arrived, far_rows = lax.optimization_barrier((odd_arrived, far_rows))
    free = jnp.zeros_like(row)
    pad = jnp.zeros((count - seq_count + 1, 2 * columns), f32)
    near = jnp.concatenate([free] + far_rows[:-1] + [free, pad], 0)
    far = jnp.concatenate([free] + far_rows + [pad], 0)

    routes = [
        (distance, parity)
        for distance in range(1, seq_count - 1)
        for parity in range(2)
        if any(
            (i // distance) % 2 == parity and (i > 0 or i + distance < seq_count - 1)
            for i in range(seq_count - distance)
        )
    ]
    routes = [route for route in routes if route != (1, 0)] + [(1, 0)]
    over = "m" * len(routes)
    pair_prev, query_next, memory, grad_memory, row_prev, *sent = call(
        functools.partial(neighbour_kernel, routes),
        sizes,
        "fppRor",
        [("p", bf16)] * 2 + [("m", bf16)] * 2 + [("o", f32)] + [("m", bf16)] * len(routes),
    )(info, even_arrived, odd_arrived, near, row, mix)
    arrived = [swapped(part, *route, lowest=1) for part, route in zip(sent, routes)]
    local_out, grad_att, stats = call(
        attend_kernel, sizes, "fpppr", (("c", f32), ("c", f32), ("s", f32))
    )(info, query, pair, pair_prev, mix)
    if by_swaps:
        all_tokens = [tokens] + [from_core(tokens, step) for step in range(1, dp_count)]
        all_tokens, stats = lax.optimization_barrier((all_tokens, stats))
        token_parts = pl.pallas_call(
            functools.partial(pack_kernel, seq_count, dp_count),
            in_specs=[SMEM_SPEC] + [VMEM_SPEC] * dp_count,
            out_specs=[VMEM_SPEC] * dp_count,
            out_shape=[jax.ShapeDtypeStruct((seq_count * part_rows, seg_len), bf16)] * dp_count,
            **limits(),
        )(info, *all_tokens)
        local_out, token_parts = lax.optimization_barrier((local_out, token_parts))
    blended, grad_query, note = call(
        functools.partial(retrieve_kernel, routes),
        sizes,
        "fpoRrccsm" + over,
        (("c", bf16), ("c", bf16), ("n", f32)),
    )(info, query, row_prev, far, mix, local_out, grad_att, stats, memory, *arrived)
    notes = [shifted(note, -step) for step in range(1, seq_count)]

    def of_cores(grad):
        return [grad] + [from_core(grad, step) for step in range(1, dp_count)]

    def row_blocks(grads):
        return pl.pallas_call(
            row_blocks_kernel,
            in_specs=[SMEM_SPEC] + [VMEM_SPEC] * (2 * dp_count),
            out_specs=[VMEM_SPEC] * 2,
            out_shape=[
                jax.ShapeDtypeStruct((seq_count, part_rows, columns), bf16),
                jax.ShapeDtypeStruct((2, part_rows, columns), bf16),
            ],
            **limits(),
        )(info, *token_parts, *grads)

    grad_scale = 1.0 / math.sqrt(seq_count * dp_count * seg_len)
    block = (part_rows, columns)
    part_shape = jax.ShapeDtypeStruct(block, bf16)
    whole = pl.BlockSpec(block, lambda i, info: (0, 0))
    first = pl.BlockSpec((1,) + block, lambda i, info: (0, 0, 0))

    def on_terms(kernel, ins, outs, out_shape, **more):
        return pl.pallas_call(
            kernel,
            grid_spec=pltpu.PrefetchScalarGridSpec(
                num_scalar_prefetch=1, grid=(1,), in_specs=ins, out_specs=outs
            ),
            out_shape=out_shape,
            **limits(**more),
        )

    def at_block(index):
        return pl.BlockSpec((1,) + block, lambda i, info: (index(info[SEQ]), 0, 0))

    def swapped_ends(first):
        last = seq_count - 1
        return lax.ppermute(first, "seq", [(0, 1), (last, last - 1)])

    def inner_messages(terms, arrived, arrays, *order):
        def inner(info_ref, *refs):
            inner_kernel(*refs[:3], *refs[-arrays:])

        size = (2 // arrays,) + block
        return on_terms(
            inner,
            [
                pl.BlockSpec((2,) + block, lambda i, info: (0, 0, 0)),
                at_block(lambda z: jnp.where(z < 2, 3, 0)),
                at_block(lambda z: jnp.where(z < 2, 2, 1)),
            ]
            + [HBM_SPEC] * len(order),
            [pl.BlockSpec(size, lambda i, info: (0, 0, 0))] * arrays,
            [jax.ShapeDtypeStruct(size, bf16)] * arrays,
        )(info, arrived, terms, terms, *order)

    def end_message(terms, far, *order):
        return on_terms(
            outer_kernel,
            [first, at_block(lambda z: lax.bitwise_xor(z, 1))] + [HBM_SPEC] * len(order),
            whole,
            part_shape,
        )(info, far, terms, *order)

    def finish(terms, even, odd, which, into=()):
        last = odd.shape[0] - 1
        odd_block = pl.BlockSpec((1,) + block, lambda i, info: (last, 0, 0))
        return on_terms(
            functools.partial(finish_kernel, grad_scale),
            [whole, odd_block, at_block(lambda z: z)] + [HBM_SPEC] * len(into),
            pl.BlockSpec((1,) + block, lambda i, info: (which, 0, 0)),
            jax.ShapeDtypeStruct((3,) + block, f32),
            input_output_aliases={4: 0} if into else {},
        )(info, even, odd, terms, *into)

    if by_swaps:
        query_terms, query_first = row_blocks(of_cores(grad_query))
        notes[0], query_terms, query_first = lax.optimization_barrier(
            (notes[0], query_terms, query_first)
        )
        notes[1:], query_first = lax.optimization_barrier((notes[1:], query_first))
        query_ends = swapped_ends(query_first)
    key_rest, grad_value = call(
        functools.partial(key_value_kernel, routes, 1),
        sizes,
        "fppnprn" + over + "m",
        (("c", f32), ("c", bf16)),
    )(info, pair, query, note, query_next, mix, notes[0], grad_memory, *arrived)
    grad_key = pl.pallas_call(
        functools.partial(join_kernel, heads),
        out_shape=jax.ShapeDtypeStruct((seg_len, columns), bf16),
        **limits(),
    )(pair, key_rest, *notes[1:])
    if not by_swaps:
        contract = (((0,), (0,)), ((), ()))

        def rows_for(core):
            return jnp.concatenate(
                [
                    lax.dynamic_slice_in_dim(
                        tokens, (block * dp_count + core) * part_rows, part_rows, 1
                    )
                    for block in range(seq_count)
                ],
                1,
            )

        token_columns = [rows_for(dp_at)] + [
            from_core(rows_for((dp_at + step) % dp_count), step) for step in range(1, dp_count)
        ]

        def summed(grad):
            grads = [grad] + [from_core(grad, step) for step in range(1, dp_count)]
            terms = sum(
                lax.dot_general(part, term, contract, preferred_element_type=f32)
                for part, term in zip(token_columns, grads)
            ).reshape(seq_count, part_rows, grad.shape[1])

            def block(index):
                index = jnp.clip(index, 0, seq_count - 1)
                return lax.dynamic_index_in_dim(terms, index, 0, False)

            ups = downs = jnp.zeros((part_rows, grad.shape[1]), bf16)
            for turn in range(1, seq_count):
                ahead = seq_count - turn
                ups = shifted((ups + block(seq_at + ahead)).astype(bf16), 1, 0, turn - 1)
                downs = shifted((downs + block(seq_at - ahead)).astype(bf16), -1, ahead)
            return ups + downs + block(seq_at)

        rows = summed(jnp.concatenate([grad_query, grad_key, grad_value], 1)) * grad_scale
        return (blended[None], rows.reshape(part_rows, 3, columns))

    values, grad_key = lax.optimization_barrier((of_cores(grad_value), grad_key))
    keys = of_cores(grad_key)
    value_terms, value_first = row_blocks(values)
    value_ends = swapped_ends(value_first)
    keys, value_terms = lax.optimization_barrier((keys, value_terms))
    key_terms, key_first = row_blocks(keys)
    key_ends = swapped_ends(key_first)

    (message,) = inner_messages(query_terms, query_ends, 1, key_terms)
    query_odd = swapped(message, 1, 1)
    (message,) = inner_messages(value_terms, value_ends, 1, message)
    value_odd = swapped(message, 1, 1)
    message = end_message(query_terms, query_odd, message)
    query_even = swapped(message, 1, 0)
    messages = inner_messages(key_terms, key_ends, 2, message)
    key_far, key_near = [swapped(message, 1, 1) for message in messages]
    message = end_message(value_terms, value_odd, query_even, *messages)
    value_even = swapped(message, 1, 0)
    message = end_message(key_terms, key_far, message)
    key_even = swapped(message, 1, 0)
    grad_weights = finish(query_terms, query_even, query_odd, 0)
    grad_weights = finish(value_terms, value_even, value_odd, 2, (grad_weights,))
    grad_weights = finish(key_terms, key_even, key_near, 1, (grad_weights,))
    return (blended[None], jnp.transpose(grad_weights, (1, 0, 2)))


def solution(mesh):
    return jax.shard_map(
        local,
        mesh=mesh,
        in_specs=(
            P("dp", "seq", None),
            P(None, "head"),
            P(None, "head"),
            P(None, "head"),
            P("head"),
            P("dp", "seq", "head"),
        ),
        out_specs=(P("dp", "seq", "head"), P(("seq", "dp"), None, "head")),
        check_vma=False,
    )
```
